256 devices in a mesh: grp: 16 (over x_lo, z), dom: 16 (over y, x_hi, core).
Axes of the slice: x: 4 (x_hi: 2, x_lo: 2; x = x_hi * 2 + x_lo), y: 4, z: 8, core: 2. Of those that a mesh axis runs over, the one named last changes fastest.
Arguments:
- features: bfloat16 [16, 16, 512, 128], P('grp', 'dom'), may hold values from -6 to 6
- w_self: bfloat16 [128, 128], replicated, may hold values from -0.5 to 0.5
- w_neigh: bfloat16 [128, 128], replicated, may hold values from -0.5 to 0.5
- out_bias: float32 [128], replicated, may hold values from -1 to 1
- adj_tiles: bfloat16 [16, 16, 16, 8, 128, 128], P('grp', 'dom')
- tile_rows: int32 [16, 16, 16, 8], P('grp', 'dom'), may hold values from 0 to 3
- tile_cols: int32 [16, 16, 16, 8], P('grp', 'dom'), may hold values from 0 to 3
- tile_count: int32 [16, 16, 16], P('grp', 'dom'), may hold values from 1 to 8, as said below
- send_rows: int32 [16, 16, 16, 256], P('grp', 'dom'), may hold values from 0 to 511
- send_count: int32 [16, 16, 16], P('grp', 'dom'), may hold values from 1 to 256, as said below
- halo_weight: float32 [16, 16, 16, 256], P('grp', 'dom'), may hold values from 0.5 to 2
- recv_rows: int32 [16, 16, 16, 256], P('grp', 'dom'), may hold values from 0 to 511
- cotangent: bfloat16 [16, 16, 512, 128], P('grp', 'dom'), may hold values from -6 to 6
Outputs:
- output: bfloat16 [16, 16, 512, 128], P('grp', 'dom')
- grad_weights: float32 [256, 128], P('grp', 'dom')
- grad_bias: float32 [128], replicated
The draws below stay inside these ranges and needn't reach their ends.
Inputs may be any that keep to these rules, and one draw needn't show every extreme that they name: tile_count[g, d, g] is 8 for every block; other counts vary from partition to partition. `send_count`: in every node-block group one partition receives 256 used slots from every other partition.
All inputs are finite; a program needn't handle non-finite values.
Results may differ from the reference program's by a relative error of at most 0.0095.
Values may be sent and summed in bfloat16 or wider, within the bound.
A program may use at most 64 MiB of HBM per device.

```python
import math
import jax
import jax.numpy as jnp
from jax import lax

FEATS = 128
UNITS = 128
TILE = 128
HALO = 256
ROW_TILES = 4
SLOTS = 8
ROWS_DEV = 512
NODES = 131072
N_GRP = 16
N_DOM = 16


def draw_adj_tiles(key, part):
    key = jax.random.fold_in(key, 7)
    first, second = jax.random.split(key)
    shape = (N_GRP, N_DOM, N_GRP, SLOTS, TILE, TILE)
    values = jax.random.uniform(first, shape, jnp.float32, 0.05, 1.0)
    present = jax.random.randint(second, shape, 0, 4) == 0
    return jnp.where(present, values, 0.0).astype(jnp.bfloat16)


def draw_tile_count(key, part):
    key = jax.random.fold_in(key, 11)
    first, second = jax.random.split(key)
    level = jax.random.randint(first, (N_GRP, N_DOM, 1), 1, 5)
    top = jnp.maximum(1, SLOTS * level // 4)
    counts = jax.random.randint(second, (N_GRP, N_DOM, N_GRP), 1, top + 1)
    own = jnp.arange(N_GRP, dtype=jnp.int32)[None, None, :] == jnp.arange(N_GRP, dtype=jnp.int32)[:, None, None]
    return jnp.where(own, SLOTS, counts).astype(jnp.int32)


def draw_send_count(key, part):
    key = jax.random.fold_in(key, 13)
    first, second = jax.random.split(key)
    counts = jax.random.randint(first, (N_GRP, N_DOM, N_DOM), 1, HALO + 1)
    target = jax.random.randint(second, (N_GRP, 1, 1), 0, N_DOM)
    full = jnp.arange(N_DOM, dtype=jnp.int32)[None, None, :] == target
    return jnp.where(full, HALO, counts).astype(jnp.int32)


def plant(result, key, smallest, high):
    place = [jax.random.randint(jax.random.fold_in(key, axis), (), 0, length) for axis, length in enumerate(result.shape)]
    longest = result.shape.index(max(result.shape))
    beside = place[:longest] + [(place[longest] + 1) % result.shape[longest]] + place[longest + 1:]
    return result.at[tuple(place)].set(smallest).at[tuple(beside)].set(high)


def with_spikes(drawn, own_key, source, target, blocks, factor):
    owner, partner = [(jnp.arange(drawn.shape[axis_at]) // (drawn.shape[axis_at] // blocks)).reshape([-1 if axis == axis_at else 1 for axis in range(drawn.ndim)]) for axis_at in (source, target)]
    chosen = jax.random.permutation(own_key, blocks)[partner]
    strong = (owner == chosen) | (owner == (partner + blocks // 2) % blocks)
    return jnp.where(strong, factor * drawn, drawn)


def level_of(rng, extent, cuts, smallest, top_value):
    def one(axis_at, blocks):
        steps = jax.random.uniform(jax.random.fold_in(jax.random.fold_in(rng, 6), axis_at), (blocks,), jnp.float32, smallest / len(cuts), top_value / len(cuts))
        return jnp.repeat(jnp.exp(steps), extent[axis_at] // blocks).reshape((-1,) + (1,) * (len(extent) - axis_at - 1))

    factor_of = one(*cuts[0])
    for cut in cuts[1:]:
        factor_of = factor_of * one(*cut)
    return factor_of


def gaussian(stream_key, extent, spread, reach, pieces=(), held_as=jnp.bfloat16):
    result = spread * jax.random.normal(stream_key, extent, jnp.float32)
    if pieces:
        result = result * level_of(stream_key, extent, pieces, -0.22, 0.18)
    return jnp.clip(result, -reach, reach).astype(held_as)


def gaussian_with(key, extent, scale, bound, cuts, heavy, kind=jnp.bfloat16):
    result = scale * jax.random.normal(key, extent, jnp.float32)
    if cuts:
        result = result * level_of(key, extent, cuts, -0.22, 0.18)
    return jnp.clip(with_spikes(result, jax.random.fold_in(key, 3), *heavy), -bound, bound).astype(kind)


def setup_inputs(seed: int = 0) -> dict:
    splits = jax.random.split(jax.random.key(seed), 14)
    features = gaussian(splits[0], (N_GRP, N_DOM, ROWS_DEV, FEATS), 1.0, 6.0, ((0, 16), (1, 16)))
    w_self = gaussian(splits[1], (FEATS, UNITS), FEATS ** -0.5, 0.5)
    w_neigh = gaussian(splits[2], (FEATS, UNITS), FEATS ** -0.5, 0.5)
    out_bias = jnp.clip(jax.random.uniform(splits[3], (UNITS,), jnp.float32, -1.0, 1.0), -1.0, 1.0)
    adj_tiles = draw_adj_tiles(jax.random.fold_in(splits[13], 71), 0)
    tile_rows = plant(jax.random.randint(splits[5], (N_GRP, N_DOM, N_GRP, SLOTS), 0, ROW_TILES), jax.random.fold_in(splits[5], 1), 0, ROW_TILES - 1).astype(jnp.int32)
    tile_cols = plant(jax.random.randint(splits[6], (N_GRP, N_DOM, N_GRP, SLOTS), 0, ROW_TILES), jax.random.fold_in(splits[6], 1), 0, ROW_TILES - 1).astype(jnp.int32)
    tile_count = draw_tile_count(jax.random.fold_in(splits[13], 71), 0)
    send_rows = plant(jax.random.randint(splits[8], (N_GRP, N_DOM, N_DOM, HALO), 0, ROWS_DEV), jax.random.fold_in(splits[8], 1), 0, ROWS_DEV - 1).astype(jnp.int32)
    send_count = draw_send_count(jax.random.fold_in(splits[13], 71), 0)
    halo_weight = jnp.clip(jnp.exp(math.log(2.0) - 1.3862944 * jax.random.uniform(splits[10], (N_GRP, N_DOM, N_DOM, HALO), jnp.float32) ** level_of(splits[10], (N_GRP, N_DOM, N_DOM, HALO), ((0, 16), (1, 16)), -0.2, 0.2)), 0.5, 2.0)
    recv_rows = plant(jax.random.randint(splits[11], (N_GRP, N_DOM, N_DOM, HALO), 0, ROWS_DEV), jax.random.fold_in(splits[11], 1), 0, ROWS_DEV - 1).astype(jnp.int32)
    cotangent = gaussian_with(splits[12], (N_GRP, N_DOM, ROWS_DEV, UNITS), 1.0, 6.0, ((0, 16), (1, 16)), (1, 3, 16, 2.0))
    return {"features": features, "w_self": w_self, "w_neigh": w_neigh, "out_bias": out_bias, "adj_tiles": adj_tiles, "tile_rows": tile_rows, "tile_cols": tile_cols, "tile_count": tile_count, "send_rows": send_rows, "send_count": send_count, "halo_weight": halo_weight, "recv_rows": recv_rows, "cotangent": cotangent}


def reference(features, w_self, w_neigh, out_bias, adj_tiles, tile_rows, tile_cols, tile_count, send_rows, send_count, halo_weight, recv_rows, cotangent):
    tile_ids = jnp.arange(ROW_TILES, dtype=jnp.int32)
    slot_ids = jnp.arange(SLOTS, dtype=jnp.int32)
    halo_ids = jnp.arange(HALO, dtype=jnp.int32)
    dom_ids = jnp.arange(N_DOM, dtype=jnp.int32)
    block_ids = jnp.arange(N_GRP, dtype=jnp.int32)
    position = jnp.arange(ROWS_DEV, dtype=jnp.int32)
    highest = lax.Precision.HIGHEST

    def device(flat):
        grp_index = flat // N_DOM
        dom_index = flat % N_DOM
        own_rows = features[grp_index, dom_index]
        partition = features[:, dom_index].reshape(N_GRP, ROW_TILES, TILE, FEATS)
        picked = partition[block_ids[:, None], tile_cols[grp_index, dom_index]]
        blocks = adj_tiles[grp_index, dom_index]
        product = jnp.einsum('bsij,bsjf->bsif', blocks.astype(jnp.float32), picked.astype(jnp.float32), precision=highest)
        placing = ((tile_rows[grp_index, dom_index][None] == tile_ids[:, None, None]) & (slot_ids[None, None, :] < tile_count[grp_index, dom_index][None, :, None])).astype(jnp.float32)
        local_sum = jnp.einsum('rbs,bsif->rif', placing, product, precision=highest).reshape(ROWS_DEV, FEATS)
        row_weight = lax.optimization_barrier(jnp.sum(blocks, axis=-1, dtype=jnp.float32))
        local_degree = jnp.einsum('rbs,bsi->ri', placing, row_weight, precision=highest).reshape(ROWS_DEV)
        group_rows = features[grp_index]
        send_idx = send_rows[grp_index][:, dom_index]
        sent_rows = group_rows[dom_ids[:, None], send_idx]
        keep = (halo_ids[None, :] < send_count[grp_index][:, dom_index][:, None]) & (dom_ids[:, None] != dom_index)
        edge_weight = jnp.where(keep, halo_weight[grp_index][:, dom_index], 0.0)
        outgoing = (edge_weight[..., None] * sent_rows.astype(jnp.float32)).astype(jnp.bfloat16)
        landing = recv_rows[grp_index, dom_index].reshape(-1)
        hits = landing[None, :] == position[:, None]
        halo_sum = jnp.dot(hits.astype(jnp.bfloat16), outgoing.reshape(-1, FEATS), preferred_element_type=jnp.float32)
        halo_degree = lax.optimization_barrier(jnp.sum(jnp.where(hits, edge_weight.reshape(-1)[None, :], 0.0), axis=1))
        aggregate = ((local_sum + halo_sum) / jnp.sqrt(1.0 + local_degree + halo_degree)[:, None]).astype(jnp.bfloat16)
        preact = jnp.dot(own_rows, w_self, preferred_element_type=jnp.float32) + jnp.dot(aggregate, w_neigh, preferred_element_type=jnp.float32) + out_bias
        sigma = jax.nn.sigmoid(preact)
        output = (preact * sigma).astype(jnp.bfloat16)
        slope = (cotangent[grp_index, dom_index].astype(jnp.float32) * sigma * (1.0 + preact * (1.0 - sigma))).astype(jnp.bfloat16)
        term_w = jnp.concatenate([jnp.einsum('nf,nh->fh', own_rows, slope, preferred_element_type=jnp.float32), jnp.einsum('nf,nh->fh', aggregate, slope, preferred_element_type=jnp.float32)], axis=0)
        term_b = lax.optimization_barrier(jnp.sum(slope.astype(jnp.float32), axis=0))
        return (output, term_w, term_b)
    outputs, terms_w, terms_b = lax.map(device, jnp.arange(N_GRP * N_DOM, dtype=jnp.int32))
    scale = 1.0 / math.sqrt(NODES)
    return (outputs.reshape(N_GRP, N_DOM, ROWS_DEV, UNITS), scale * lax.optimization_barrier(jnp.sum(terms_w, axis=0)), scale * lax.optimization_barrier(jnp.sum(terms_b, axis=0)))
```

```python
import math

import jax
import jax.numpy as jnp
from jax import lax
from jax.experimental import pallas as pl
from jax.experimental.pallas import tpu as pltpu
from jax.sharding import PartitionSpec as P

MESH = pl.DeviceIdType.MESH
ROWS, FEATS, TILE, SLOTS, HALO = 512, 128, 128, 8, 256
HALF = ROWS // 2
NZ = 8
PAY = FEATS + 16
BF16, F32 = jnp.bfloat16, jnp.float32


def kernel(
    feat, adj, cot, wself, wneigh, bias, trows, tcols, tcount, srows, scount, hweight, rrows,
    out, gw, gb,
    part, adjv, cotv, stage, xcat, acc, xt, hsend, hrecv, prhs, outv, catv, tbuf, rec1, tb2, rec2, tposed,
    lsem, asend, arecv, hss, hrs, p1s, p1r, p2s, p2r,
):
    g, d = lax.axis_index("grp"), lax.axis_index("dom")
    xl, z = g // NZ, lax.rem(g, NZ)
    y, xh, core = d // 4, lax.rem(d // 2, 2), lax.rem(d, 2)
    up = xl * NZ + lax.rem(z + 1, NZ)
    down = xl * NZ + lax.rem(z + NZ - 1, NZ)
    side = (1 - xl) * NZ + z

    def dom_to(j):
        dy, dx, dc = j // 4, lax.rem(j // 2, 2), lax.rem(j, 2)
        return lax.rem(y + dy, 4) * 4 + lax.rem(xh + dx, 2) * 2 + lax.rem(core + dc, 2)

    def dom_from(j):
        dy, dx, dc = j // 4, lax.rem(j // 2, 2), lax.rem(j, 2)
        return lax.rem(y + 4 - dy, 4) * 4 + lax.rem(xh + dx, 2) * 2 + lax.rem(core + dc, 2)

    def grp_to(j):
        dx, dz = j // NZ, lax.rem(j, NZ)
        return lax.rem(xl + dx, 2) * NZ + lax.rem(z + dz, NZ)

    load_x = pltpu.make_async_copy(feat, part.at[0], lsem.at[0])
    load_a = pltpu.make_async_copy(adj, adjv, lsem.at[1])
    load_c = pltpu.make_async_copy(cot, cotv, lsem.at[2])
    load_x.start()
    load_a.start()
    load_c.start()

    barrier = pltpu.get_barrier_semaphore()

    @pl.loop(1, 16)
    def _(j):
        pl.semaphore_signal(barrier, inc=1, device_id=(grp_to(j), d), device_id_type=MESH)
        pl.semaphore_signal(barrier, inc=1, device_id=(g, dom_to(j)), device_id_type=MESH)

    load_x.wait()
    xt[...] = part[0].T
    acc[...] = jnp.zeros_like(acc)
    xcat[:, FEATS:] = jnp.ones((SLOTS * TILE, FEATS), BF16)

    node = lax.broadcasted_iota(jnp.int32, (ROWS, HALO), 0)
    lane = lax.broadcasted_iota(jnp.int32, (1, HALO), 1)

    def build_halo(j):
        to = dom_to(j)
        pick = jnp.where(node == srows[pl.ds(to, 1), :], 1.0, 0.0).astype(BF16)
        weight = jnp.where(lane < scount[0, to], hweight[pl.ds(to, 1), :], 0.0)
        rows = jnp.dot(xt[...], pick, preferred_element_type=F32)
        hsend[j, 0:FEATS, :] = (rows * weight).astype(BF16)
        hsend[j, FEATS:PAY, :] = jnp.broadcast_to(weight, (PAY - FEATS, HALO)).astype(BF16)

    def halo_copy(j):
        return pltpu.make_async_remote_copy(
            src_ref=hsend.at[j], dst_ref=hrecv.at[j], send_sem=hss.at[j], recv_sem=hrs.at[j],
            device_id=(g, dom_to(j)), device_id_type=MESH,
        )

    sent = []

    def send(slot_from, slot_to, h, to):
        n = len(sent)
        copy = pltpu.make_async_remote_copy(
            src_ref=part.at[slot_from, pl.ds(h * HALF, HALF), :],
            dst_ref=part.at[slot_to, pl.ds(h * HALF, HALF), :],
            send_sem=asend.at[n], recv_sem=arecv.at[2 * slot_to + h],
            device_id=(to, d), device_id_type=MESH,
        )
        copy.start()
        sent.append(copy)

    def landed(slot, h):
        pltpu.make_async_remote_copy(
            src_ref=part.at[slot, pl.ds(h * HALF, HALF), :],
            dst_ref=part.at[slot, pl.ds(h * HALF, HALF), :],
            send_sem=asend.at[0], recv_sem=arecv.at[2 * slot + h],
            device_id=(up, d), device_id_type=MESH,
        ).wait_recv()

    def absorb(slot, source):
        stage[...] = part[slot].reshape(4, TILE, FEATS)
        for s in range(SLOTS):
            xcat[s * TILE:(s + 1) * TILE, 0:FEATS] = stage[tcols[source, s]]
        limit = jnp.full((16, TILE), tcount[0, source], jnp.int32)
        for r in range(4):
            kept = []
            for s in range(SLOTS):
                target = jnp.full((16, TILE), trows[source, s], jnp.int32)
                on = jnp.where((target == r) & (limit > s), 1.0, 0.0).astype(BF16)
                kept.append(adjv[source, s] * jnp.concatenate([on] * (TILE // 16), axis=0))
            acc[r * TILE:(r + 1) * TILE, :] += jnp.dot(
                jnp.concatenate(kept, axis=1), xcat[...], preferred_element_type=F32
            )

    def absorb_step(first, count, dist):
        def body(k, _):
            source = lax.rem(xl + k // 2, 2) * NZ + lax.rem(z + NZ + dist * (2 * lax.rem(k, 2) - 1), NZ)
            absorb(first + k, source)
            return 0
        lax.fori_loop(0, count, body, 0)

    def take_halo(lo, hi):
        def body(j, _):
            halo_copy(j).wait_recv()
            source = dom_from(j)
            prhs[0:FEATS, :] = hrecv[j, 0:FEATS, :]
            weights = hrecv[j, FEATS:PAY, :]
            for i in range(FEATS // 16):
                prhs[FEATS + 16 * i:FEATS + 16 * (i + 1), :] = weights
            hits = jnp.where(node == rrows[pl.ds(source, 1), :], 1.0, 0.0).astype(BF16)
            acc[...] += lax.dot_general(
                hits, prhs[...], (((1,), (1,)), ((), ())), preferred_element_type=F32
            )
            return 0
        lax.fori_loop(lo, hi, body, 0)

    pl.semaphore_wait(barrier, 30)

    send(0, 1, 1, side)
    send(0, 2, 0, up)
    send(0, 3, 0, down)
    send(0, 2, 1, up)
    send(0, 3, 1, down)
    send(0, 1, 0, side)

    @pl.loop(1, 16)
    def _(j):
        build_halo(j)
        halo_copy(j).start()

    landed(1, 1)
    send(1, 4, 1, up)
    send(1, 5, 1, down)
    load_a.wait()
    for dist in (1, 2):
        a = 4 * dist - 2
        landed(a, 0)
        send(a, a + 4, 0, up)
        send(a, a + 2, 0, side)
        landed(a + 1, 0)
        send(a + 1, a + 5, 0, down)
        send(a + 1, a + 3, 0, side)
        landed(a, 1)
        send(a, a + 4, 1, up)
        landed(a + 1, 1)
        send(a + 1, a + 5, 1, down)
        landed(a + 2, 1)
        send(a + 2, a + 6, 1, up)
        landed(a + 3, 1)
        send(a + 3, a + 7, 1, down)
        if dist == 1:
            landed(1, 0)
            absorb(0, g)
            absorb(1, side)
        else:
            landed(4, 0)
            landed(5, 0)
            absorb_step(2, 4, 1)
    landed(10, 0)
    send(10, 14, 0, up)
    send(10, 12, 0, side)
    landed(11, 0)
    send(11, 13, 0, side)
    landed(10, 1)
    landed(11, 1)
    send(11, 14, 1, down)
    landed(12, 1)
    send(12, 15, 1, up)
    landed(13, 1)
    landed(8, 0)
    landed(9, 0)
    absorb_step(6, 4, 2)
    take_halo(1, 6)
    landed(14, 0)
    send(14, 15, 0, side)
    landed(12, 0)
    landed(13, 0)
    absorb_step(10, 4, 3)
    take_halo(6, 16)
    landed(14, 1)
    landed(15, 1)
    landed(15, 0)
    absorb_step(14, 1, 4)
    absorb(15, lax.rem(xl + 1, 2) * NZ + lax.rem(z + 4, NZ))

    load_c.wait()
    wcat = jnp.concatenate([wself[...], wneigh[...]], axis=0)
    bias_row = bias[...]
    total_b = jnp.zeros((1, FEATS), F32)
    total_w = jnp.zeros((FEATS, 2 * FEATS), F32)
    for r in range(4):
        rs = pl.ds(r * TILE, TILE)
        agg = (acc[rs, 0:FEATS] * lax.rsqrt(1.0 + acc[rs, FEATS:])).astype(BF16)
        cat = jnp.concatenate([part[0, rs, :], agg], axis=1)
        pre = jnp.dot(cat, wcat, preferred_element_type=F32) + bias_row
        sig = jax.nn.sigmoid(pre)
        outv[rs, :] = (pre * sig).astype(BF16)
        slope = (cotv[rs, :].astype(F32) * sig * (1.0 + pre * (1.0 - sig))).astype(BF16)
        total_b += jnp.sum(slope.astype(F32), axis=0, keepdims=True)
        total_w += lax.dot_general(slope, cat, (((0,), (0,)), ((), ())), preferred_element_type=F32)
    store_o = pltpu.make_async_copy(outv, out, lsem.at[3])
    store_o.start()
    tbuf[:, 0:8, :] = total_w[:, 0:FEATS].reshape(16, 8, FEATS)
    tbuf[:, 8:16, :] = total_w[:, FEATS:].reshape(16, 8, FEATS)
    tbuf[:, 16:24, :] = jnp.broadcast_to(total_b[None], (16, 8, FEATS))

    def first_copy(j):
        return pltpu.make_async_remote_copy(
            src_ref=tbuf.at[dom_to(j)], dst_ref=rec1.at[j], send_sem=p1s.at[j], recv_sem=p1r.at[j],
            device_id=(g, dom_to(j)), device_id_type=MESH,
        )

    def second_copy(j):
        return pltpu.make_async_remote_copy(
            src_ref=tb2.at[grp_to(j) // NZ], dst_ref=rec2.at[j], send_sem=p2s.at[j], recv_sem=p2r.at[j],
            device_id=(grp_to(j), d), device_id_type=MESH,
        )

    @pl.loop(1, 16)
    def _(j):
        first_copy(j).start()

    for copy in sent:
        copy.wait_send()

    @pl.loop(1, 16)
    def _(j):
        halo_copy(j).wait_send()

    def add1(j, total):
        first_copy(j).wait_recv()
        return total + rec1[j]

    red = lax.fori_loop(1, 16, add1, tbuf[d])
    tb2[0, 0:8, :] = red[0:8]
    tb2[1, 0:8, :] = red[8:16]
    tb2[0, 8:16, :] = red[16:24]
    tb2[1, 8:16, :] = red[16:24]

    @pl.loop(1, 16)
    def _(j):
        second_copy(j).start()

    def add2(j, total):
        second_copy(j).wait_recv()
        return total + rec2[j]

    fin = lax.fori_loop(1, 16, add2, tb2[xl])
    scale = 1.0 / math.sqrt(ROWS * 256)
    tposed[...] = jnp.transpose(fin[0:8] * scale)
    gw[...] = tposed[pl.ds(pl.multiple_of(z * 16, 16), 16), :]
    gb[...] = fin[8:9] * scale

    @pl.loop(1, 16)
    def _(j):
        first_copy(j).wait_send()
        second_copy(j).wait_send()

    store_o.wait()


def local(
    features, w_self, w_neigh, out_bias, adj_tiles, tile_rows, tile_cols, tile_count, send_rows,
    send_count, halo_weight, recv_rows, cotangent,
):
    vmem = pl.BlockSpec(memory_space=pltpu.VMEM)
    smem = pl.BlockSpec(memory_space=pltpu.SMEM)
    hbm = pl.BlockSpec(memory_space=pl.ANY)
    dma = pltpu.SemaphoreType.DMA
    out, gw, gb = pl.pallas_call(
        kernel,
        out_shape=(
            jax.ShapeDtypeStruct((ROWS, FEATS), BF16),
            jax.ShapeDtypeStruct((16, 8), F32),
            jax.ShapeDtypeStruct((1, FEATS), F32),
        ),
        in_specs=[hbm, hbm, hbm, vmem, vmem, vmem, smem, smem, smem, vmem, smem, vmem, vmem],
        out_specs=(hbm, vmem, vmem),
        scratch_shapes=[
            pltpu.VMEM((16, ROWS, FEATS), BF16),
            pltpu.VMEM((16, SLOTS, TILE, TILE), BF16),
            pltpu.VMEM((ROWS, FEATS), BF16),
            pltpu.VMEM((4, TILE, FEATS), BF16),
            pltpu.VMEM((SLOTS * TILE, 2 * FEATS), BF16),
            pltpu.VMEM((ROWS, 2 * FEATS), F32),
            pltpu.VMEM((FEATS, ROWS), BF16),
            pltpu.VMEM((16, PAY, HALO), BF16),
            pltpu.VMEM((16, PAY, HALO), BF16),
            pltpu.VMEM((2 * FEATS, HALO), BF16),
            pltpu.VMEM((ROWS, FEATS), BF16),
            pltpu.VMEM((ROWS, 2 * FEATS), BF16),
            pltpu.VMEM((16, 24, FEATS), F32),
            pltpu.VMEM((16, 24, FEATS), F32),
            pltpu.VMEM((2, 16, FEATS), F32),
            pltpu.VMEM((16, 16, FEATS), F32),
            pltpu.VMEM((FEATS, 8), F32),
            dma((4,)), dma((40,)), dma((32,)), dma((16,)), dma((16,)), dma((16,)), dma((16,)), dma((16,)), dma((16,)),
        ],
        compiler_params=pltpu.CompilerParams(
            collective_id=0, has_side_effects=True, vmem_limit_bytes=48 * 1024 * 1024
        ),
    )(
        features.reshape(ROWS, FEATS),
        adj_tiles.reshape(16, SLOTS, TILE, TILE),
        cotangent.reshape(ROWS, FEATS),
        w_self,
        w_neigh,
        out_bias.reshape(1, FEATS),
        tile_rows.reshape(16, SLOTS),
        tile_cols.reshape(16, SLOTS),
        tile_count.reshape(1, 16),
        send_rows.reshape(16, HALO),
        send_count.reshape(1, 16),
        halo_weight.reshape(16, HALO),
        recv_rows.reshape(16, HALO),
    )
    return out.reshape(1, 1, ROWS, FEATS), gw, gb.reshape(FEATS)


def solution(mesh):
    placed = (
        P("grp", "dom", None, None),
        P(),
        P(),
        P(),
        P("grp", "dom", None, None, None, None),
        P("grp", "dom", None, None),
        P("grp", "dom", None, None),
        P("grp", "dom", None),
        P("grp", "dom", None, None),
        P("grp", "dom", None),
        P("grp", "dom", None, None),
        P("grp", "dom", None, None),
        P("grp", "dom", None, None),
    )
    return jax.shard_map(
        local,
        mesh=mesh,
        in_specs=placed,
        out_specs=(P("grp", "dom", None, None), P("grp", "dom"), P()),
        check_vma=False,
    )
```

```python
import math

import jax
import jax.numpy as jnp
from jax import lax
from jax.experimental import pallas as pl
from jax.experimental.pallas import tpu as pltpu
from jax.sharding import PartitionSpec as P

MESH = pl.DeviceIdType.MESH
ROWS, FEATS, TILE, SLOTS, HALO = 512, 128, 128, 8, 256
HALF = ROWS // 2
NZ = 8
PAY = FEATS + 16
BF16, F32 = jnp.bfloat16, jnp.float32


def dom_hops(j):
    dy, dx = j // 4, (j // 2) % 2
    return min(dy, 4 - dy) + 2 * dx


def grp_hops(j):
    dx, dz = j // NZ, j % NZ
    return min(dz, NZ - dz) + dx


DOM_FAR = sorted(range(1, 16), key=lambda j: -dom_hops(j))
GRP_FAR = sorted(range(1, 16), key=lambda j: -grp_hops(j))


def kernel(
    feat, adj, cot_in, wself_in, wneigh_in, bias_in, trows_in, tcols_in, tcount_in, srows_in, scount_in, hweight_in,
    rrows_in,
    out, gw, gb,
    wself, wneigh, bias, trows, tcols, tcount, srows, scount, hweight, rrows,
    part, adjv, cot, stage, xcat, acc, xt, hsend, hrecv, prhs, tbuf, rec1, tb2, rec2, wmask, fx, fxt, prows, pweight,
    lsem, asend, arecv, hss, hrs, p1s, p1r, p2s, p2r, xs, xr,
):
    g, d = lax.axis_index("grp"), lax.axis_index("dom")
    xl, z = g // NZ, lax.rem(g, NZ)
    y, xh, core = d // 4, lax.rem(d // 2, 2), lax.rem(d, 2)
    up = xl * NZ + lax.rem(z + 1, NZ)
    down = xl * NZ + lax.rem(z + NZ - 1, NZ)
    side = (1 - xl) * NZ + z
    across = y * 4 + (1 - xh) * 2 + core

    def dom_to(j):
        dy, dx, dc = j // 4, lax.rem(j // 2, 2), lax.rem(j, 2)
        return lax.rem(y + dy, 4) * 4 + lax.rem(xh + dx, 2) * 2 + lax.rem(core + dc, 2)

    def grp_to(j):
        dx, dz = j // NZ, lax.rem(j, NZ)
        return lax.rem(xl + dx, 2) * NZ + lax.rem(z + dz, NZ)

    def halo_to(q):
        return lax.rem(y + q // 2, 4) * 4 + xh * 2 + lax.rem(core + lax.rem(q, 2), 2)

    def halo_from(slot):
        q = lax.rem(slot, 8)
        return lax.rem(y + 4 - q // 2, 4) * 4 + lax.rem(xh + slot // 8, 2) * 2 + lax.rem(core + lax.rem(q, 2), 2)

    def load(n, source, target):
        copy = pltpu.make_async_copy(source, target, lsem.at[n])
        copy.start()
        return copy

    load_x = load(0, feat, part.at[0])
    load_h = [load(1, srows_in, srows), load(2, scount_in, scount), load(3, hweight_in, hweight)]
    load_t = [load(4, trows_in, trows), load(5, tcols_in, tcols), load(6, tcount_in, tcount)]
    load_a = load(7, adj, adjv)
    load_r = load(8, rrows_in, rrows)
    load_w = [load(9, wself_in, wself), load(10, wneigh_in, wneigh), load(11, bias_in, bias), load(12, cot_in, cot)]

    barrier = pltpu.get_barrier_semaphore()
    for q in (4, 5, 2, 3, 6, 7, 1):
        pl.semaphore_signal(barrier, inc=1, device_id=(g, halo_to(q)), device_id_type=MESH)
    pl.semaphore_signal(barrier, inc=1, device_id=(g, across), device_id_type=MESH)
    for to in (up, down, side):
        pl.semaphore_signal(barrier, inc=1, device_id=(to, d), device_id_type=MESH)

    for copy in load_h:
        copy.wait()
    lane = lax.broadcasted_iota(jnp.int32, (1, HALO), 1)
    for j in range(16):
        wmask[j:j + 1, :] = jnp.where(lane < scount[0, j], hweight[j:j + 1, :], 0.0)
    load_x.wait()
    xt[...] = part[0].T
    acc[...] = jnp.zeros_like(acc)
    xcat[:, FEATS:] = jnp.ones((SLOTS * TILE, FEATS), BF16)
    node = lax.broadcasted_iota(jnp.int32, (ROWS, HALO), 0)

    def build_halo(block, table, weights, to, target):
        pick = jnp.where(node == table[pl.ds(to, 1), :], 1.0, 0.0).astype(BF16)
        weight = weights[pl.ds(to, 1), :]
        rows = jnp.dot(block[...], pick, preferred_element_type=F32)
        target[0:FEATS, :] = (rows * weight).astype(BF16)
        target[FEATS:PAY, :] = jnp.broadcast_to(weight, (PAY - FEATS, HALO)).astype(BF16)

    def halo_copy(slot):
        return pltpu.make_async_remote_copy(
            src_ref=hsend.at[slot], dst_ref=hrecv.at[slot], send_sem=hss.at[slot], recv_sem=hrs.at[slot],
            device_id=(g, halo_to(lax.rem(slot, 8))), device_id_type=MESH,
        )

    def across_copy(n, source, target):
        return pltpu.make_async_remote_copy(
            src_ref=source, dst_ref=target, send_sem=xs.at[n], recv_sem=xr.at[n],
            device_id=(g, across), device_id_type=MESH,
        )

    sent = []

    def send(slot_from, slot_to, h, to):
        n = len(sent)
        copy = pltpu.make_async_remote_copy(
            src_ref=part.at[slot_from, pl.ds(h * HALF, HALF), :],
            dst_ref=part.at[slot_to, pl.ds(h * HALF, HALF), :],
            send_sem=asend.at[n], recv_sem=arecv.at[2 * slot_to + h],
            device_id=(to, d), device_id_type=MESH,
        )
        copy.start()
        sent.append(copy)

    def landed(slot, h):
        pltpu.make_async_remote_copy(
            src_ref=part.at[slot, pl.ds(h * HALF, HALF), :],
            dst_ref=part.at[slot, pl.ds(h * HALF, HALF), :],
            send_sem=asend.at[0], recv_sem=arecv.at[2 * slot + h],
            device_id=(up, d), device_id_type=MESH,
        ).wait_recv()

    def absorb(slot, source):
        stage[...] = part[slot].reshape(4, TILE, FEATS)
        for s in range(SLOTS):
            xcat[s * TILE:(s + 1) * TILE, 0:FEATS] = stage[tcols[s, source]]
        limit = jnp.full((16, TILE), tcount[0, source], jnp.int32)
        for r in range(4):
            kept = []
            for s in range(SLOTS):
                target = jnp.full((16, TILE), trows[s, source], jnp.int32)
                on = jnp.where((target == r) & (limit > s), 1.0, 0.0).astype(BF16)
                kept.append(adjv[source, s] * jnp.concatenate([on] * (TILE // 16), axis=0))
            acc[r * TILE:(r + 1) * TILE, :] += jnp.dot(
                jnp.concatenate(kept, axis=1), xcat[...], preferred_element_type=F32
            )

    def absorb_step(first, count, dist):
        def body(k, _):
            source = lax.rem(xl + k // 2, 2) * NZ + lax.rem(z + NZ + dist * (2 * lax.rem(k, 2) - 1), NZ)
            absorb(first + k, source)
            return 0
        lax.fori_loop(0, count, body, 0)

    def take_halo(slot):
        source = halo_from(slot)
        prhs[0:FEATS, :] = hrecv[slot, 0:FEATS, :]
        weights = hrecv[slot, FEATS:PAY, :]
        for i in range(FEATS // 16):
            prhs[FEATS + 16 * i:FEATS + 16 * (i + 1), :] = weights
        hits = jnp.where(node == rrows[pl.ds(source, 1), :], 1.0, 0.0).astype(BF16)
        acc[...] += lax.dot_general(hits, prhs[...], (((1,), (1,)), ((), ())), preferred_element_type=F32)

    def take_halos(lo, hi):
        def body(slot, _):
            halo_copy(slot).wait_recv()
            take_halo(slot)
            return 0
        lax.fori_loop(lo, hi, body, 0)

    pl.semaphore_wait(barrier, 11)

    send(0, 1, 1, side)
    send(0, 2, 0, up)
    send(0, 3, 0, down)
    crossing = [
        across_copy(0, srows, prows), across_copy(1, wmask, pweight), across_copy(2, part.at[0], fx),
    ]
    for copy in crossing:
        copy.start()
    send(0, 2, 1, up)
    send(0, 3, 1, down)
    send(0, 1, 0, side)

    @pl.loop(1, 8)
    def _(q):
        build_halo(xt, srows, wmask, halo_to(q), hsend.at[q])
        halo_copy(q).start()

    landed(1, 1)
    send(1, 4, 1, up)
    send(1, 5, 1, down)
    load_a.wait()
    load_r.wait()
    for copy in load_t:
        copy.wait()
    for dist in (1, 2):
        a = 4 * dist - 2
        landed(a, 0)
        send(a, a + 4, 0, up)
        send(a, a + 2, 0, side)
        landed(a + 1, 0)
        send(a + 1, a + 5, 0, down)
        send(a + 1, a + 3, 0, side)
        landed(a, 1)
        send(a, a + 4, 1, up)
        landed(a + 1, 1)
        send(a + 1, a + 5, 1, down)
        landed(a + 2, 1)
        send(a + 2, a + 6, 1, up)
        landed(a + 3, 1)
        send(a + 3, a + 7, 1, down)
        if dist == 1:
            for copy in crossing:
                copy.wait_recv()
            fxt[...] = fx[...].T

            @pl.loop(1, 8)
            def _(q):
                build_halo(fxt, prows, pweight, halo_to(q), hsend.at[8 + q])
                halo_copy(8 + q).start()

            build_halo(fxt, prows, pweight, halo_to(0), hrecv.at[8])
            landed(1, 0)
            absorb(0, g)
            absorb(1, side)
        else:
            landed(4, 0)
            landed(5, 0)
            absorb_step(2, 4, 1)
            take_halo(8)
    landed(10, 0)
    send(10, 14, 0, up)
    send(10, 12, 0, side)
    landed(11, 0)
    send(11, 13, 0, side)
    landed(10, 1)
    landed(11, 1)
    send(11, 14, 1, down)
    landed(12, 1)
    send(12, 15, 1, up)
    landed(13, 1)
    landed(8, 0)
    landed(9, 0)
    absorb_step(6, 4, 2)
    take_halos(1, 5)
    landed(14, 0)
    send(14, 15, 0, side)
    landed(12, 0)
    landed(13, 0)
    absorb_step(10, 4, 3)
    take_halos(5, 8)
    landed(14, 1)
    absorb_step(14, 1, 4)
    take_halos(9, 16)
    landed(15, 1)
    landed(15, 0)
    absorb(15, lax.rem(xl + 1, 2) * NZ + lax.rem(z + 4, NZ))

    for copy in load_w:
        copy.wait()
    wcat = jnp.concatenate([wself[...], wneigh[...]], axis=0)
    bias_row = bias[...]
    total_b = jnp.zeros((1, FEATS), F32)
    total_w = jnp.zeros((FEATS, 2 * FEATS), F32)
    for r in range(4):
        rs = pl.ds(r * TILE, TILE)
        agg = (acc[rs, 0:FEATS] * lax.rsqrt(1.0 + acc[rs, FEATS:])).astype(BF16)
        cat = jnp.concatenate([part[0, rs, :], agg], axis=1)
        pre = jnp.dot(cat, wcat, preferred_element_type=F32) + bias_row
        sig = jax.nn.sigmoid(pre)
        out[rs, :] = (pre * sig).astype(BF16)
        slope = (cot[rs, :].astype(F32) * sig * (1.0 + pre * (1.0 - sig))).astype(BF16)
        total_b += jnp.sum(slope.astype(F32), axis=0, keepdims=True)
        total_w += lax.dot_general(slope, cat, (((0,), (0,)), ((), ())), preferred_element_type=F32)
    tbuf[:, 0:8, :] = total_w[:, 0:FEATS].reshape(16, 8, FEATS)
    tbuf[:, 8:16, :] = total_w[:, FEATS:].reshape(16, 8, FEATS)
    tbuf[:, 16:24, :] = jnp.broadcast_to(total_b[None], (16, 8, FEATS))

    def first_copy(j):
        return pltpu.make_async_remote_copy(
            src_ref=tbuf.at[dom_to(j), pl.ds(0, 17), :], dst_ref=rec1.at[j, pl.ds(0, 17), :],
            send_sem=p1s.at[j], recv_sem=p1r.at[j],
            device_id=(g, dom_to(j)), device_id_type=MESH,
        )

    def second_copy(j):
        return pltpu.make_async_remote_copy(
            src_ref=tb2.at[grp_to(j), pl.ds(0, 2), :], dst_ref=rec2.at[j, pl.ds(0, 2), :],
            send_sem=p2s.at[j], recv_sem=p2r.at[j],
            device_id=(grp_to(j), d), device_id_type=MESH,
        )

    for j in DOM_FAR:
        first_copy(j).start()

    for copy in sent + crossing:
        copy.wait_send()

    @pl.loop(1, 8)
    def _(q):
        halo_copy(q).wait_send()
        halo_copy(8 + q).wait_send()

    red_w, red_b = tbuf[d, 0:16, :], tbuf[d, 16:17, :]
    for j in DOM_FAR[::-1]:
        first_copy(j).wait_recv()
        red_w += rec1[j, 0:16, :]
        red_b += rec1[j, 16:17, :]

    row8 = lax.broadcasted_iota(jnp.int32, (8, FEATS), 0)
    block16 = lax.broadcasted_iota(jnp.int32, (8, FEATS), 1) // 16
    for half in range(2):
        tile = red_w[8 * half:8 * half + 8]
        turned = jnp.zeros((8, FEATS), F32)
        for k in range(8):
            moved = tile if k == 0 else pltpu.roll(tile, 16 * k, 1)
            moved = jnp.where(row8 == block16, moved, 0.0)
            turned += moved if k == 0 else pltpu.roll(moved, 8 - k, 0)
        for p in range(8):
            tb2[8 * half + p, 0:1, :] = turned[p:p + 1]
            tb2[8 * half + p, 1:2, :] = red_b
    for j in GRP_FAR:
        second_copy(j).start()
    fin = tb2[g, 0:2, :]
    for j in GRP_FAR[::-1]:
        second_copy(j).wait_recv()
        fin += rec2[j, 0:2, :]
    fin *= 1.0 / math.sqrt(ROWS * 256)
    for c in range(8):
        gw[c:c + 1, :] = fin[0:1, 16 * c:16 * c + 16]
    gb[...] = fin[1:2]

    @pl.loop(1, 16)
    def _(j):
        first_copy(j).wait_send()
        second_copy(j).wait_send()


def local(
    features, w_self, w_neigh, out_bias, adj_tiles, tile_rows, tile_cols, tile_count, send_rows,
    send_count, halo_weight, recv_rows, cotangent,
):
    hbm = pl.BlockSpec(memory_space=pltpu.HBM)
    vmem = pl.BlockSpec(memory_space=pltpu.VMEM)
    dma = pltpu.SemaphoreType.DMA
    out, gw, gb = pl.pallas_call(
        kernel,
        out_shape=(
            jax.ShapeDtypeStruct((ROWS, FEATS), BF16),
            jax.ShapeDtypeStruct((8, 16), F32),
            jax.ShapeDtypeStruct((1, FEATS), F32),
        ),
        in_specs=[hbm] * 13,
        out_specs=(vmem, vmem, vmem),
        scratch_shapes=[
            pltpu.VMEM((FEATS, FEATS), BF16),
            pltpu.VMEM((FEATS, FEATS), BF16),
            pltpu.VMEM((1, FEATS), F32),
            pltpu.SMEM((SLOTS, 16), jnp.int32),
            pltpu.SMEM((SLOTS, 16), jnp.int32),
            pltpu.SMEM((1, 16), jnp.int32),
            pltpu.VMEM((16, HALO), jnp.int32),
            pltpu.SMEM((1, 16), jnp.int32),
            pltpu.VMEM((16, HALO), F32),
            pltpu.VMEM((16, HALO), jnp.int32),
            pltpu.VMEM((16, ROWS, FEATS), BF16),
            pltpu.VMEM((16, SLOTS, TILE, TILE), BF16),
            pltpu.VMEM((ROWS, FEATS), BF16),
            pltpu.VMEM((4, TILE, FEATS), BF16),
            pltpu.VMEM((SLOTS * TILE, 2 * FEATS), BF16),
            pltpu.VMEM((ROWS, 2 * FEATS), F32),
            pltpu.VMEM((FEATS, ROWS), BF16),
            pltpu.VMEM((16, PAY, HALO), BF16),
            pltpu.VMEM((16, PAY, HALO), BF16),
            pltpu.VMEM((2 * FEATS, HALO), BF16),
            pltpu.VMEM((16, 24, FEATS), F32),
            pltpu.VMEM((16, 24, FEATS), F32),
            pltpu.VMEM((16, 8, FEATS), F32),
            pltpu.VMEM((16, 8, FEATS), F32),
            pltpu.VMEM((16, HALO), F32),
            pltpu.VMEM((ROWS, FEATS), BF16),
            pltpu.VMEM((FEATS, ROWS), BF16),
            pltpu.VMEM((16, HALO), jnp.int32),
            pltpu.VMEM((16, HALO), F32),
            dma((16,)), dma((40,)), dma((32,)), dma((16,)), dma((16,)), dma((16,)), dma((16,)), dma((16,)), dma((16,)),
            dma((3,)), dma((3,)),
        ],
        compiler_params=pltpu.CompilerParams(
            collective_id=0, has_side_effects=True, vmem_limit_bytes=40 * 1024 * 1024
        ),
    )(*(pltpu.with_memory_space_constraint(value, pltpu.HBM) for value in (
        features.reshape(ROWS, FEATS),
        adj_tiles.reshape(16, SLOTS, TILE, TILE),
        cotangent.reshape(ROWS, FEATS),
        w_self,
        w_neigh,
        out_bias.reshape(1, FEATS),
        tile_rows.reshape(16, SLOTS).T,
        tile_cols.reshape(16, SLOTS).T,
        tile_count.reshape(1, 16),
        send_rows.reshape(16, HALO),
        send_count.reshape(1, 16),
        halo_weight.reshape(16, HALO),
        recv_rows.reshape(16, HALO),
    )))
    return out.reshape(1, 1, ROWS, FEATS), gw.T, gb.reshape(FEATS)


def solution(mesh):
    placed = (
        P("grp", "dom", None, None),
        P(),
        P(),
        P(),
        P("grp", "dom", None, None, None, None),
        P("grp", "dom", None, None),
        P("grp", "dom", None, None),
        P("grp", "dom", None),
        P("grp", "dom", None, None),
        P("grp", "dom", None),
        P("grp", "dom", None, None),
        P("grp", "dom", None, None),
        P("grp", "dom", None, None),
    )
    return jax.shard_map(
        local,
        mesh=mesh,
        in_specs=placed,
        out_specs=(P("grp", "dom", None, None), P("grp", "dom"), P()),
        check_vma=False,
    )
```

```python
import math

import jax
import jax.numpy as jnp
from jax import lax
from jax.experimental import pallas as pl
from jax.experimental.pallas import tpu as pltpu
from jax.sharding import PartitionSpec as P

MESH = pl.DeviceIdType.MESH
ROWS, FEATS, TILE, SLOTS, HALO = 512, 128, 128, 8, 256
HALF = ROWS // 2
NZ = 8
PAY = FEATS + 16
BF16, F32 = jnp.bfloat16, jnp.float32


def dom_hops(j):
    dy, dx = j // 4, (j // 2) % 2
    return min(dy, 4 - dy) + 2 * dx


def grp_hops(j):
    dx, dz = j // NZ, j % NZ
    return min(dz, NZ - dz) + dx


DOM_FAR = sorted(range(1, 16), key=lambda j: -dom_hops(j))
GRP_FAR = sorted(range(1, 16), key=lambda j: -grp_hops(j))
PIECES = ((0, HALF), (HALF, HALF), (HALF, HALF // 2), (HALF + HALF // 2, HALF // 2))


def kernel(
    feat, adj, cot_in, wself_in, wneigh_in, bias_in, trows_in, tcols_in, tcount_in, srows_in, scount_in, hweight_in,
    rrows_in,
    out, gw, gb,
    wself, wneigh, bias, trows, tcols, tcount, srows, scount, hweight, rrows,
    part, adjv, cot, stage, acc, xt, hsend, hrecv, prhs, tbuf, rec1, tb2, rec2, wmask, fx, fxt, prows, pweight, table, plan, segment, degree,
    lsem, asend, arecv, hss, hrs, p1s, p1r, p2s, p2r, xs, xr,
):
    g, d = lax.axis_index("grp"), lax.axis_index("dom")
    xl, z = g // NZ, lax.rem(g, NZ)
    y, xh, core = d // 4, lax.rem(d // 2, 2), lax.rem(d, 2)
    up = xl * NZ + lax.rem(z + 1, NZ)
    down = xl * NZ + lax.rem(z + NZ - 1, NZ)
    side = (1 - xl) * NZ + z
    across = y * 4 + (1 - xh) * 2 + core

    def dom_to(j):
        dy, dx, dc = j // 4, lax.rem(j // 2, 2), lax.rem(j, 2)
        return lax.rem(y + dy, 4) * 4 + lax.rem(xh + dx, 2) * 2 + lax.rem(core + dc, 2)

    def grp_to(j):
        dx, dz = j // NZ, lax.rem(j, NZ)
        return lax.rem(xl + dx, 2) * NZ + lax.rem(z + dz, NZ)

    def halo_to(q):
        return lax.rem(y + q // 2, 4) * 4 + xh * 2 + lax.rem(core + lax.rem(q, 2), 2)

    def halo_from(slot):
        q = lax.rem(slot, 8)
        return lax.rem(y + 4 - q // 2, 4) * 4 + lax.rem(xh + slot // 8, 2) * 2 + lax.rem(core + lax.rem(q, 2), 2)

    def load(n, source, target):
        copy = pltpu.make_async_copy(source, target, lsem.at[n])
        copy.start()
        return copy

    load_x = load(0, feat, part.at[0])
    load_h = [load(1, srows_in, srows), load(2, scount_in, scount), load(3, hweight_in, hweight)]
    load_t = [load(4, trows_in, trows), load(5, tcols_in, tcols), load(6, tcount_in, tcount)]
    load_a = load(7, adj, adjv)
    load_r = load(8, rrows_in, rrows)
    load_w = [load(9, wself_in, wself), load(10, wneigh_in, wneigh), load(11, bias_in, bias), load(12, cot_in, cot)]

    barrier = pltpu.get_barrier_semaphore()
    for q in (4, 5, 2, 3, 6, 7, 1):
        pl.semaphore_signal(barrier, inc=1, device_id=(g, halo_to(q)), device_id_type=MESH)
    pl.semaphore_signal(barrier, inc=1, device_id=(g, across), device_id_type=MESH)
    for to in (up, down, side):
        pl.semaphore_signal(barrier, inc=1, device_id=(to, d), device_id_type=MESH)

    for copy in load_h:
        copy.wait()
    lane = lax.broadcasted_iota(jnp.int32, (1, HALO), 1)
    for j in range(16):
        wmask[j:j + 1, :] = jnp.where(lane < scount[0, j], hweight[j:j + 1, :], 0.0)
    load_x.wait()
    xt[...] = part[0].T
    acc[...] = jnp.zeros_like(acc)
    segment[8] = jnp.zeros((TILE, FEATS), F32)
    degree[...] = jnp.zeros((TILE, FEATS), F32)
    node = lax.broadcasted_iota(jnp.int32, (ROWS, HALO), 0)

    def build_halo(block, table, weights, to, target):
        pick = jnp.where(node == table[pl.ds(to, 1), :], 1.0, 0.0).astype(BF16)
        weight = weights[pl.ds(to, 1), :]
        rows = jnp.dot(block[...], pick, preferred_element_type=F32)
        target[0:FEATS, :] = (rows * weight).astype(BF16)
        target[FEATS:PAY, :] = jnp.broadcast_to(weight, (PAY - FEATS, HALO)).astype(BF16)

    def halo_copy(slot):
        return pltpu.make_async_remote_copy(
            src_ref=hsend.at[slot], dst_ref=hrecv.at[slot], send_sem=hss.at[slot], recv_sem=hrs.at[slot],
            device_id=(g, halo_to(lax.rem(slot, 8))), device_id_type=MESH,
        )

    def across_copy(n, source, target):
        return pltpu.make_async_remote_copy(
            src_ref=source, dst_ref=target, send_sem=xs.at[n], recv_sem=xr.at[n],
            device_id=(g, across), device_id_type=MESH,
        )

    sent = []

    def send(slot_from, slot_to, piece, to):
        n = len(sent)
        rows = pl.ds(*PIECES[piece])
        copy = pltpu.make_async_remote_copy(
            src_ref=part.at[slot_from, rows, :], dst_ref=part.at[slot_to, rows, :],
            send_sem=asend.at[n], recv_sem=arecv.at[4 * slot_to + piece],
            device_id=(to, d), device_id_type=MESH,
        )
        copy.start()
        sent.append(copy)

    def landed(slot, piece):
        rows = pl.ds(*PIECES[piece])
        pltpu.make_async_remote_copy(
            src_ref=part.at[slot, rows, :], dst_ref=part.at[slot, rows, :],
            send_sem=asend.at[0], recv_sem=arecv.at[4 * slot + piece],
            device_id=(up, d), device_id_type=MESH,
        ).wait_recv()

    def sort_slots():
        count = tcount[...]
        keys = [jnp.where(count > s, trows[s:s + 1, :], 4) for s in range(SLOTS)]
        one = jnp.ones((1, 16), jnp.int32)
        none = jnp.zeros((1, 16), jnp.int32)
        rank = []
        for s in range(SLOTS):
            total = none
            for t in range(SLOTS):
                if t != s:
                    ahead = keys[t] <= keys[s] if t < s else keys[t] < keys[s]
                    total += jnp.where(ahead, one, none)
            rank.append(total)
        for i in range(SLOTS):
            at, column, key = none, none, none
            for s in range(SLOTS):
                here = rank[s] == i
                at += jnp.where(here, s * one, none)
                column += jnp.where(here, tcols[s:s + 1, :], none)
                key += jnp.where(here, keys[s], none)
            table[i:i + 1, :] = at
            table[8 + i:9 + i, :] = column
            table[16 + i:17 + i, :] = key
        for r in range(4):
            upto, equal = none, none
            for s in range(SLOTS):
                upto += jnp.where(keys[s] <= r, one, none)
                equal += jnp.where(keys[s] == r, one, none)
            table[24 + r:25 + r, :] = jnp.where(equal > 0, upto - 1, 8)
        copy = pltpu.make_async_copy(table, plan, lsem.at[13])
        copy.start()
        return copy

    lane16 = lax.broadcasted_iota(jnp.int32, (16, FEATS), 1)

    def absorb(slot, source):
        stage[...] = part[slot].reshape(4, TILE, FEATS)
        running, before, tiles, marks = None, None, [], []
        for i in range(SLOTS):
            tile = adjv[source, plan[i, source]]
            product = jnp.dot(tile, stage[plan[8 + i, source]], preferred_element_type=F32)
            key = jnp.full((16, FEATS), plan[16 + i, source], jnp.int32)
            tiles.append(tile)
            marks += [jnp.where(lane16 == key, 1.0, 0.0).astype(BF16)] * (TILE // 16)
            if i:
                same = jnp.concatenate([jnp.where(key == before, 1, 0)] * (TILE // 16), axis=0) > 0
                product += jnp.where(same, running, 0.0)
            running, before = product, key
            segment[i] = running
        degree[...] += jnp.dot(
            jnp.concatenate(tiles, axis=1), jnp.concatenate(marks, axis=0), preferred_element_type=F32
        )
        for r in range(4):
            acc[r * TILE:(r + 1) * TILE, 0:FEATS] += segment[plan[24 + r, source]]

    def absorb_pair(first, dist, column):
        def body(k, _):
            absorb(first + k, column * NZ + lax.rem(z + NZ + dist * (2 * k - 1), NZ))
            return 0
        lax.fori_loop(0, 2, body, 0)

    def take_halo(slot):
        source = halo_from(slot)
        prhs[0:FEATS, :] = hrecv[slot, 0:FEATS, :]
        weights = hrecv[slot, FEATS:PAY, :]
        for i in range(FEATS // 16):
            prhs[FEATS + 16 * i:FEATS + 16 * (i + 1), :] = weights
        hits = jnp.where(node == rrows[pl.ds(source, 1), :], 1.0, 0.0).astype(BF16)
        acc[...] += lax.dot_general(hits, prhs[...], (((1,), (1,)), ((), ())), preferred_element_type=F32)

    def take_halos(lo, hi):
        def body(slot, _):
            halo_copy(slot).wait_recv()
            take_halo(slot)
            return 0
        lax.fori_loop(lo, hi, body, 0)

    pl.semaphore_wait(barrier, 11)

    send(0, 1, 1, side)
    send(0, 2, 0, up)
    send(0, 3, 0, down)
    crossing = [
        across_copy(0, srows, prows), across_copy(1, wmask, pweight), across_copy(2, part.at[0], fx),
    ]
    for copy in crossing:
        copy.start()
    send(0, 2, 1, up)
    send(0, 3, 1, down)
    send(0, 1, 0, side)

    @pl.loop(1, 8)
    def _(q):
        build_halo(xt, srows, wmask, halo_to(q), hsend.at[q])
        halo_copy(q).start()

    for copy in load_t:
        copy.wait()
    planned = sort_slots()
    other = 1 - xl
    landed(2, 0)
    send(2, 6, 0, up)
    send(2, 4, 0, side)
    landed(3, 0)
    send(3, 7, 0, down)
    send(3, 5, 0, side)
    landed(1, 1)
    send(1, 4, 1, up)
    send(1, 5, 1, down)
    load_a.wait()
    load_r.wait()
    planned.wait()
    absorb(0, g)
    landed(2, 1)
    send(2, 6, 1, up)
    landed(3, 1)
    send(3, 7, 1, down)
    for copy in crossing:
        copy.wait_recv()
    fxt[...] = fx[...].T

    @pl.loop(1, 8)
    def _(q):
        build_halo(fxt, prows, pweight, halo_to(q), hsend.at[8 + q])
        halo_copy(8 + q).start()

    landed(6, 0)
    send(6, 10, 0, up)
    send(6, 8, 0, side)
    landed(7, 0)
    send(7, 11, 0, down)
    send(7, 9, 0, side)
    absorb_pair(2, 1, xl)
    landed(4, 1)
    send(4, 8, 1, up)
    landed(5, 1)
    send(5, 9, 1, down)
    landed(1, 0)
    absorb(1, side)
    build_halo(fxt, prows, pweight, halo_to(0), hrecv.at[8])
    take_halo(8)
    landed(6, 1)
    send(6, 10, 1, up)
    landed(7, 1)
    send(7, 11, 1, down)
    absorb_pair(6, 2, xl)
    landed(10, 0)
    send(10, 14, 0, up)
    send(10, 12, 0, side)
    landed(11, 0)
    send(11, 13, 0, side)
    landed(4, 0)
    landed(5, 0)
    absorb_pair(4, 1, other)
    landed(8, 1)
    send(8, 12, 1, up)
    landed(9, 1)
    send(9, 13, 1, down)
    take_halos(1, 5)
    landed(10, 1)
    landed(11, 1)
    send(11, 14, 1, down)
    absorb_pair(10, 3, xl)
    landed(14, 0)
    send(14, 15, 0, side)
    landed(8, 0)
    landed(9, 0)
    absorb_pair(8, 2, other)
    landed(12, 1)
    send(12, 15, 2, up)
    landed(13, 1)
    send(13, 15, 3, down)
    landed(14, 1)
    absorb(14, xl * NZ + lax.rem(z + 4, NZ))
    take_halos(5, 8)
    take_halos(9, 16)
    landed(12, 0)
    landed(13, 0)
    absorb_pair(12, 3, other)
    landed(15, 2)
    landed(15, 3)
    landed(15, 0)
    absorb(15, other * NZ + lax.rem(z + 4, NZ))

    for copy in load_w:
        copy.wait()
    wcat = jnp.concatenate([wself[...], wneigh[...]], axis=0)
    bias_row = bias[...]
    total_b = jnp.zeros((1, FEATS), F32)
    total_w = jnp.zeros((FEATS, 2 * FEATS), F32)
    for r in range(4):
        rs = pl.ds(r * TILE, TILE)
        total = 1.0 + acc[rs, FEATS:] + jnp.broadcast_to(degree[:, r:r + 1], (TILE, FEATS))
        agg = (acc[rs, 0:FEATS] * lax.rsqrt(total)).astype(BF16)
        cat = jnp.concatenate([part[0, rs, :], agg], axis=1)
        pre = jnp.dot(cat, wcat, preferred_element_type=F32) + bias_row
        sig = jax.nn.sigmoid(pre)
        out[rs, :] = (pre * sig).astype(BF16)
        slope = (cot[rs, :].astype(F32) * sig * (1.0 + pre * (1.0 - sig))).astype(BF16)
        total_b += jnp.sum(slope.astype(F32), axis=0, keepdims=True)
        total_w += lax.dot_general(slope, cat, (((0,), (0,)), ((), ())), preferred_element_type=F32)
    tbuf[:, 0:8, :] = total_w[:, 0:FEATS].reshape(16, 8, FEATS)
    tbuf[:, 8:16, :] = total_w[:, FEATS:].reshape(16, 8, FEATS)
    tbuf[:, 16:24, :] = jnp.broadcast_to(total_b[None], (16, 8, FEATS))

    def first_copy(j):
        return pltpu.make_async_remote_copy(
            src_ref=tbuf.at[dom_to(j), pl.ds(0, 17), :], dst_ref=rec1.at[j, pl.ds(0, 17), :],
            send_sem=p1s.at[j], recv_sem=p1r.at[j],
            device_id=(g, dom_to(j)), device_id_type=MESH,
        )

    def second_copy(j):
        return pltpu.make_async_remote_copy(
            src_ref=tb2.at[grp_to(j), pl.ds(0, 2), :], dst_ref=rec2.at[j, pl.ds(0, 2), :],
            send_sem=p2s.at[j], recv_sem=p2r.at[j],
            device_id=(grp_to(j), d), device_id_type=MESH,
        )

    for j in DOM_FAR:
        first_copy(j).start()

    for copy in sent + crossing:
        copy.wait_send()

    @pl.loop(1, 8)
    def _(q):
        halo_copy(q).wait_send()
        halo_copy(8 + q).wait_send()

    red_w, red_b = tbuf[d, 0:16, :], tbuf[d, 16:17, :]
    for j in DOM_FAR[::-1]:
        first_copy(j).wait_recv()
        red_w += rec1[j, 0:16, :]
        red_b += rec1[j, 16:17, :]

    row8 = lax.broadcasted_iota(jnp.int32, (8, FEATS), 0)
    block16 = lax.broadcasted_iota(jnp.int32, (8, FEATS), 1) // 16
    for half in range(2):
        tile = red_w[8 * half:8 * half + 8]
        turned = jnp.zeros((8, FEATS), F32)
        for k in range(8):
            moved = tile if k == 0 else pltpu.roll(tile, 16 * k, 1)
            moved = jnp.where(row8 == block16, moved, 0.0)
            turned += moved if k == 0 else pltpu.roll(moved, 8 - k, 0)
        for p in range(8):
            tb2[8 * half + p, 0:1, :] = turned[p:p + 1]
            tb2[8 * half + p, 1:2, :] = red_b
    for j in GRP_FAR:
        second_copy(j).start()
    fin = tb2[g, 0:2, :]
    for j in GRP_FAR[::-1]:
        second_copy(j).wait_recv()
        fin += rec2[j, 0:2, :]
    fin *= 1.0 / math.sqrt(ROWS * 256)
    for c in range(8):
        gw[c:c + 1, :] = fin[0:1, 16 * c:16 * c + 16]
    gb[...] = fin[1:2]

    @pl.loop(1, 16)
    def _(j):
        first_copy(j).wait_send()
        second_copy(j).wait_send()


def local(
    features, w_self, w_neigh, out_bias, adj_tiles, tile_rows, tile_cols, tile_count, send_rows,
    send_count, halo_weight, recv_rows, cotangent,
):
    hbm = pl.BlockSpec(memory_space=pltpu.HBM)
    vmem = pl.BlockSpec(memory_space=pltpu.VMEM)
    dma = pltpu.SemaphoreType.DMA
    out, gw, gb = pl.pallas_call(
        kernel,
        out_shape=(
            jax.ShapeDtypeStruct((ROWS, FEATS), BF16),
            jax.ShapeDtypeStruct((8, 16), F32),
            jax.ShapeDtypeStruct((1, FEATS), F32),
        ),
        in_specs=[hbm] * 13,
        out_specs=(vmem, vmem, vmem),
        scratch_shapes=[
            pltpu.VMEM((FEATS, FEATS), BF16),
            pltpu.VMEM((FEATS, FEATS), BF16),
            pltpu.VMEM((1, FEATS), F32),
            pltpu.VMEM((SLOTS, 16), jnp.int32),
            pltpu.VMEM((SLOTS, 16), jnp.int32),
            pltpu.VMEM((1, 16), jnp.int32),
            pltpu.VMEM((16, HALO), jnp.int32),
            pltpu.SMEM((1, 16), jnp.int32),
            pltpu.VMEM((16, HALO), F32),
            pltpu.VMEM((16, HALO), jnp.int32),
            pltpu.VMEM((16, ROWS, FEATS), BF16),
            pltpu.VMEM((16, SLOTS, TILE, TILE), BF16),
            pltpu.VMEM((ROWS, FEATS), BF16),
            pltpu.VMEM((4, TILE, FEATS), BF16),
            pltpu.VMEM((ROWS, 2 * FEATS), F32),
            pltpu.VMEM((FEATS, ROWS), BF16),
            pltpu.VMEM((16, PAY, HALO), BF16),
            pltpu.VMEM((16, PAY, HALO), BF16),
            pltpu.VMEM((2 * FEATS, HALO), BF16),
            pltpu.VMEM((16, 24, FEATS), F32),
            pltpu.VMEM((16, 24, FEATS), F32),
            pltpu.VMEM((16, 8, FEATS), F32),
            pltpu.VMEM((16, 8, FEATS), F32),
            pltpu.VMEM((16, HALO), F32),
            pltpu.VMEM((ROWS, FEATS), BF16),
            pltpu.VMEM((FEATS, ROWS), BF16),
            pltpu.VMEM((16, HALO), jnp.int32),
            pltpu.VMEM((16, HALO), F32),
            pltpu.VMEM((32, 16), jnp.int32),
            pltpu.SMEM((32, 16), jnp.int32),
            pltpu.VMEM((9, TILE, FEATS), F32),
            pltpu.VMEM((TILE, FEATS), F32),
            dma((16,)), dma((40,)), dma((64,)), dma((16,)), dma((16,)), dma((16,)), dma((16,)), dma((16,)), dma((16,)),
            dma((3,)), dma((3,)),
        ],
        compiler_params=pltpu.CompilerParams(
            collective_id=0, has_side_effects=True, vmem_limit_bytes=40 * 1024 * 1024
        ),
    )(*(pltpu.with_memory_space_constraint(value, pltpu.HBM) for value in (
        features.reshape(ROWS, FEATS),
        adj_tiles.reshape(16, SLOTS, TILE, TILE),
        cotangent.reshape(ROWS, FEATS),
        w_self,
        w_neigh,
        out_bias.reshape(1, FEATS),
        tile_rows.reshape(16, SLOTS).T,
        tile_cols.reshape(16, SLOTS).T,
        tile_count.reshape(1, 16),
        send_rows.reshape(16, HALO),
        send_count.reshape(1, 16),
        halo_weight.reshape(16, HALO),
        recv_rows.reshape(16, HALO),
    )))
    return out.reshape(1, 1, ROWS, FEATS), gw.T, gb.reshape(FEATS)


def solution(mesh):
    placed = (
        P("grp", "dom", None, None),
        P(),
        P(),
        P(),
        P("grp", "dom", None, None, None, None),
        P("grp", "dom", None, None),
        P("grp", "dom", None, None),
        P("grp", "dom", None),
        P("grp", "dom", None, None),
        P("grp", "dom", None),
        P("grp", "dom", None, None),
        P("grp", "dom", None, None),
        P("grp", "dom", None, None),
    )
    return jax.shard_map(
        local,
        mesh=mesh,
        in_specs=placed,
        out_specs=(P("grp", "dom", None, None), P("grp", "dom"), P()),
        check_vma=False,
    )
```

```python
import math

import jax
import jax.numpy as jnp
from jax import lax
from jax.experimental import pallas as pl
from jax.experimental.pallas import tpu as pltpu
from jax.sharding import PartitionSpec as P

MESH = pl.DeviceIdType.MESH
ROWS, FEATS, TILE, SLOTS, HALO = 512, 128, 128, 8, 256
HALF = ROWS // 2
NZ = 8
PAY = FEATS + 16
BF16, F32 = jnp.bfloat16, jnp.float32


def dom_hops(j):
    dy, dx = j // 4, (j // 2) % 2
    return min(dy, 4 - dy) + 2 * dx


def grp_hops(j):
    dx, dz = j // NZ, j % NZ
    return min(dz, NZ - dz) + dx


DOM_FAR = sorted(range(1, 16), key=lambda j: -dom_hops(j))
GRP_FAR = sorted(range(1, 16), key=lambda j: -grp_hops(j))
PIECES = ((0, HALF), (HALF, HALF), (HALF, HALF // 2), (HALF + HALF // 2, HALF // 2))


def kernel(
    feat, adj, cot_in, wself_in, wneigh_in, bias_in, trows_in, tcols_in, tcount_in, srows_in, scount_in, hweight_in,
    rrows_in,
    out, gw, gb,
    wself, wneigh, bias, trows, tcols, tcount, srows, scount, hweight, rrows,
    part, adjv, cot, stage, acc, xt, hsend, hrecv, tbuf, rec1, tb2, rec2, wmask, fx, fxt, prows, pweight, table, plan, segment, degree,
    lsem, asend, arecv, hss, hrs, p1s, p1r, p2s, p2r, xs, xr,
):
    g, d = lax.axis_index("grp"), lax.axis_index("dom")
    xl, z = g // NZ, lax.rem(g, NZ)
    y, xh, core = d // 4, lax.rem(d // 2, 2), lax.rem(d, 2)
    up = xl * NZ + lax.rem(z + 1, NZ)
    down = xl * NZ + lax.rem(z + NZ - 1, NZ)
    side = (1 - xl) * NZ + z
    across = y * 4 + (1 - xh) * 2 + core

    def dom_to(j):
        dy, dx, dc = j // 4, lax.rem(j // 2, 2), lax.rem(j, 2)
        return lax.rem(y + dy, 4) * 4 + lax.rem(xh + dx, 2) * 2 + lax.rem(core + dc, 2)

    def grp_to(j):
        dx, dz = j // NZ, lax.rem(j, NZ)
        return lax.rem(xl + dx, 2) * NZ + lax.rem(z + dz, NZ)

    def halo_to(q):
        return lax.rem(y + q // 2, 4) * 4 + xh * 2 + lax.rem(core + lax.rem(q, 2), 2)

    def halo_from(slot):
        q = lax.rem(slot, 8)
        return lax.rem(y + 4 - q // 2, 4) * 4 + lax.rem(xh + slot // 8, 2) * 2 + lax.rem(core + lax.rem(q, 2), 2)

    def load(n, source, target):
        copy = pltpu.make_async_copy(source, target, lsem.at[n])
        copy.start()
        return copy

    load_x = load(0, feat, part.at[0])
    load_h = [load(1, srows_in, srows), load(2, scount_in, scount), load(3, hweight_in, hweight)]
    load_t = [load(4, trows_in, trows), load(5, tcols_in, tcols), load(6, tcount_in, tcount)]
    load_a = load(7, adj, adjv)
    load_r = load(8, rrows_in, rrows)
    load_w = [load(9, wself_in, wself), load(10, wneigh_in, wneigh), load(11, bias_in, bias), load(12, cot_in, cot)]

    barrier = pltpu.get_barrier_semaphore()
    for q in (4, 5, 2, 3, 6, 7, 1):
        pl.semaphore_signal(barrier, inc=1, device_id=(g, halo_to(q)), device_id_type=MESH)
    pl.semaphore_signal(barrier, inc=1, device_id=(g, across), device_id_type=MESH)
    for to in (up, down, side):
        pl.semaphore_signal(barrier, inc=1, device_id=(to, d), device_id_type=MESH)

    for copy in load_h:
        copy.wait()
    lane = lax.broadcasted_iota(jnp.int32, (1, HALO), 1)
    for j in range(16):
        wmask[j:j + 1, :] = jnp.where(lane < scount[0, j], hweight[j:j + 1, :], 0.0)
    load_x.wait()
    xt[...] = part[0].T
    acc[...] = jnp.zeros_like(acc)
    segment[8] = jnp.zeros((TILE, FEATS), F32)
    degree[...] = jnp.zeros((TILE, FEATS), F32)
    node = lax.broadcasted_iota(jnp.int32, (ROWS, HALO), 0)

    def build_halo(block, table, weights, to, target):
        pick = jnp.where(node == table[pl.ds(to, 1), :], 1.0, 0.0).astype(BF16)
        weight = weights[pl.ds(to, 1), :]
        rows = jnp.dot(block[...], pick, preferred_element_type=F32)
        target[0:FEATS, :] = (rows * weight).astype(BF16)
        target[FEATS:PAY, :] = jnp.broadcast_to(weight, (PAY - FEATS, HALO)).astype(BF16)

    def halo_copy(slot):
        return pltpu.make_async_remote_copy(
            src_ref=hsend.at[slot], dst_ref=hrecv.at[slot], send_sem=hss.at[slot], recv_sem=hrs.at[slot],
            device_id=(g, halo_to(lax.rem(slot, 8))), device_id_type=MESH,
        )

    def across_copy(n, source, target):
        return pltpu.make_async_remote_copy(
            src_ref=source, dst_ref=target, send_sem=xs.at[n], recv_sem=xr.at[n],
            device_id=(g, across), device_id_type=MESH,
        )

    sent = []

    def send(slot_from, slot_to, piece, to):
        n = len(sent)
        rows = pl.ds(*PIECES[piece])
        copy = pltpu.make_async_remote_copy(
            src_ref=part.at[slot_from, rows, :], dst_ref=part.at[slot_to, rows, :],
            send_sem=asend.at[n], recv_sem=arecv.at[4 * slot_to + piece],
            device_id=(to, d), device_id_type=MESH,
        )
        copy.start()
        sent.append(copy)

    def landed(slot, piece):
        rows = pl.ds(*PIECES[piece])
        pltpu.make_async_remote_copy(
            src_ref=part.at[slot, rows, :], dst_ref=part.at[slot, rows, :],
            send_sem=asend.at[0], recv_sem=arecv.at[4 * slot + piece],
            device_id=(up, d), device_id_type=MESH,
        ).wait_recv()

    def sort_slots():
        count = tcount[...]
        keys = [jnp.where(count > s, trows[s:s + 1, :], 4) for s in range(SLOTS)]
        one = jnp.ones((1, 16), jnp.int32)
        none = jnp.zeros((1, 16), jnp.int32)
        rank = []
        for s in range(SLOTS):
            total = none
            for t in range(SLOTS):
                if t != s:
                    ahead = keys[t] <= keys[s] if t < s else keys[t] < keys[s]
                    total += jnp.where(ahead, one, none)
            rank.append(total)
        for i in range(SLOTS):
            at, column, key = none, none, none
            for s in range(SLOTS):
                here = rank[s] == i
                at += jnp.where(here, s * one, none)
                column += jnp.where(here, tcols[s:s + 1, :], none)
                key += jnp.where(here, keys[s], none)
            table[i:i + 1, :] = at
            table[8 + i:9 + i, :] = column
            table[16 + i:17 + i, :] = key
        for r in range(4):
            upto, equal = none, none
            for s in range(SLOTS):
                upto += jnp.where(keys[s] <= r, one, none)
                equal += jnp.where(keys[s] == r, one, none)
            table[24 + r:25 + r, :] = jnp.where(equal > 0, upto - 1, 8)
        copy = pltpu.make_async_copy(table, plan, lsem.at[13])
        copy.start()
        return copy

    lane16 = lax.broadcasted_iota(jnp.int32, (16, FEATS), 1)

    def absorb(slot, source):
        stage[...] = part[slot].reshape(4, TILE, FEATS)
        running, before, tiles, marks = None, None, [], []
        for i in range(SLOTS):
            tile = adjv[source, plan[i, source]]
            product = jnp.dot(tile, stage[plan[8 + i, source]], preferred_element_type=F32)
            key = jnp.full((16, FEATS), plan[16 + i, source], jnp.int32)
            tiles.append(tile)
            marks += [jnp.where(lane16 == key, 1.0, 0.0).astype(BF16)] * (TILE // 16)
            if i:
                same = jnp.concatenate([jnp.where(key == before, 1, 0)] * (TILE // 16), axis=0) > 0
                product += jnp.where(same, running, 0.0)
            running, before = product, key
            segment[i] = running
        degree[...] += jnp.dot(
            jnp.concatenate(tiles, axis=1), jnp.concatenate(marks, axis=0), preferred_element_type=F32
        )
        for r in range(4):
            acc[r * TILE:(r + 1) * TILE, 0:FEATS] += segment[plan[24 + r, source]]

    def absorb_pair(first, dist, column):
        def body(k, _):
            absorb(first + k, column * NZ + lax.rem(z + NZ + dist * (2 * k - 1), NZ))
            return 0
        lax.fori_loop(0, 2, body, 0)

    def take_halo(*slots):
        for slot in slots:
            if slot != 8:
                halo_copy(slot).wait_recv()
        hits = jnp.concatenate(
            [jnp.where(node == rrows[pl.ds(halo_from(slot), 1), :], 1.0, 0.0).astype(BF16) for slot in slots], axis=1
        )
        rows = jnp.concatenate([hrecv[slot] for slot in slots], axis=1)
        acc[:, 0:PAY] += lax.dot_general(hits, rows, (((1,), (1,)), ((), ())), preferred_element_type=F32)

    pl.semaphore_wait(barrier, 11)

    send(0, 1, 1, side)
    send(0, 2, 0, up)
    send(0, 3, 0, down)
    crossing = [
        across_copy(0, srows, prows), across_copy(1, wmask, pweight), across_copy(2, part.at[0], fx),
    ]
    for copy in crossing:
        copy.start()
    send(0, 2, 1, up)
    send(0, 3, 1, down)
    send(0, 1, 0, side)

    @pl.loop(1, 8)
    def _(q):
        build_halo(xt, srows, wmask, halo_to(q), hsend.at[q])
        halo_copy(q).start()

    for copy in load_t:
        copy.wait()
    planned = sort_slots()
    other = 1 - xl
    landed(2, 0)
    send(2, 6, 0, up)
    send(2, 4, 0, side)
    landed(3, 0)
    send(3, 7, 0, down)
    send(3, 5, 0, side)
    landed(1, 1)
    send(1, 4, 1, up)
    send(1, 5, 1, down)
    load_a.wait()
    load_r.wait()
    planned.wait()
    absorb(0, g)
    landed(2, 1)
    send(2, 6, 1, up)
    landed(3, 1)
    send(3, 7, 1, down)
    for copy in crossing:
        copy.wait_recv()
    fxt[...] = fx[...].T

    @pl.loop(1, 8)
    def _(q):
        build_halo(fxt, prows, pweight, halo_to(q), hsend.at[8 + q])
        halo_copy(8 + q).start()

    landed(6, 0)
    send(6, 10, 0, up)
    send(6, 8, 0, side)
    landed(7, 0)
    send(7, 11, 0, down)
    send(7, 9, 0, side)
    absorb_pair(2, 1, xl)
    landed(4, 1)
    send(4, 8, 1, up)
    landed(5, 1)
    send(5, 9, 1, down)
    landed(1, 0)
    absorb(1, side)
    build_halo(fxt, prows, pweight, halo_to(0), hrecv.at[8])
    landed(6, 1)
    send(6, 10, 1, up)
    landed(7, 1)
    send(7, 11, 1, down)
    absorb_pair(6, 2, xl)
    take_halo(1, 2)
    landed(10, 0)
    send(10, 14, 0, up)
    send(10, 12, 0, side)
    landed(11, 0)
    send(11, 13, 0, side)
    landed(4, 0)
    landed(5, 0)
    absorb_pair(4, 1, other)
    take_halo(3, 4)
    landed(8, 1)
    send(8, 12, 1, up)
    landed(9, 1)
    send(9, 13, 1, down)
    take_halo(5, 6)
    take_halo(7, 8)
    landed(10, 1)
    landed(11, 1)
    send(11, 14, 1, down)
    absorb_pair(10, 3, xl)
    take_halo(9, 10)
    landed(14, 0)
    send(14, 15, 0, side)
    landed(8, 0)
    landed(9, 0)
    absorb_pair(8, 2, other)
    take_halo(11, 12)
    landed(12, 1)
    send(12, 15, 2, up)
    landed(13, 1)
    send(13, 15, 3, down)
    landed(14, 1)
    absorb(14, xl * NZ + lax.rem(z + 4, NZ))
    take_halo(13, 14)
    landed(12, 0)
    landed(13, 0)
    absorb_pair(12, 3, other)
    take_halo(15)
    landed(15, 2)
    landed(15, 3)
    landed(15, 0)
    absorb(15, other * NZ + lax.rem(z + 4, NZ))

    for copy in load_w:
        copy.wait()
    wcat = jnp.concatenate([wself[...], wneigh[...]], axis=0)
    bias_row = bias[...]
    total_b = jnp.zeros((1, FEATS), F32)
    total_w = jnp.zeros((FEATS, 2 * FEATS), F32)
    for r in range(4):
        rs = pl.ds(r * TILE, TILE)
        total = jnp.broadcast_to(1.0 + acc[rs, FEATS:FEATS + 1] + degree[:, r:r + 1], (TILE, FEATS))
        agg = (acc[rs, 0:FEATS] * lax.rsqrt(total)).astype(BF16)
        cat = jnp.concatenate([part[0, rs, :], agg], axis=1)
        pre = jnp.dot(cat, wcat, preferred_element_type=F32) + bias_row
        sig = jax.nn.sigmoid(pre)
        out[rs, :] = (pre * sig).astype(BF16)
        slope = (cot[rs, :].astype(F32) * sig * (1.0 + pre * (1.0 - sig))).astype(BF16)
        total_b += jnp.sum(slope.astype(F32), axis=0, keepdims=True)
        total_w += lax.dot_general(slope, cat, (((0,), (0,)), ((), ())), preferred_element_type=F32)
    tbuf[:, 0:8, :] = total_w[:, 0:FEATS].reshape(16, 8, FEATS)
    tbuf[:, 8:16, :] = total_w[:, FEATS:].reshape(16, 8, FEATS)
    tbuf[:, 16:24, :] = jnp.broadcast_to(total_b[None], (16, 8, FEATS))

    def first_copy(j):
        return pltpu.make_async_remote_copy(
            src_ref=tbuf.at[dom_to(j), pl.ds(0, 17), :], dst_ref=rec1.at[j, pl.ds(0, 17), :],
            send_sem=p1s.at[j], recv_sem=p1r.at[j],
            device_id=(g, dom_to(j)), device_id_type=MESH,
        )

    def second_copy(j):
        return pltpu.make_async_remote_copy(
            src_ref=tb2.at[grp_to(j), pl.ds(0, 2), :], dst_ref=rec2.at[j, pl.ds(0, 2), :],
            send_sem=p2s.at[j], recv_sem=p2r.at[j],
            device_id=(grp_to(j), d), device_id_type=MESH,
        )

    for j in DOM_FAR:
        first_copy(j).start()

    for copy in sent + crossing:
        copy.wait_send()

    @pl.loop(1, 8)
    def _(q):
        halo_copy(q).wait_send()
        halo_copy(8 + q).wait_send()

    red_w, red_b = tbuf[d, 0:16, :], tbuf[d, 16:17, :]
    for j in DOM_FAR[::-1]:
        first_copy(j).wait_recv()
        red_w += rec1[j, 0:16, :]
        red_b += rec1[j, 16:17, :]

    row8 = lax.broadcasted_iota(jnp.int32, (8, FEATS), 0)
    block16 = lax.broadcasted_iota(jnp.int32, (8, FEATS), 1) // 16
    for half in range(2):
        tile = red_w[8 * half:8 * half + 8]
        turned = jnp.zeros((8, FEATS), F32)
        for k in range(8):
            moved = tile if k == 0 else pltpu.roll(tile, 16 * k, 1)
            moved = jnp.where(row8 == block16, moved, 0.0)
            turned += moved if k == 0 else pltpu.roll(moved, 8 - k, 0)
        for p in range(8):
            tb2[8 * half + p, 0:1, :] = turned[p:p + 1]
            tb2[8 * half + p, 1:2, :] = red_b
    for j in GRP_FAR:
        second_copy(j).start()
    fin = tb2[g, 0:2, :]
    for j in GRP_FAR[::-1]:
        second_copy(j).wait_recv()
        fin += rec2[j, 0:2, :]
    fin *= 1.0 / math.sqrt(ROWS * 256)
    for c in range(8):
        gw[c:c + 1, :] = fin[0:1, 16 * c:16 * c + 16]
    gb[...] = fin[1:2]

    @pl.loop(1, 16)
    def _(j):
        first_copy(j).wait_send()
        second_copy(j).wait_send()


def local(
    features, w_self, w_neigh, out_bias, adj_tiles, tile_rows, tile_cols, tile_count, send_rows,
    send_count, halo_weight, recv_rows, cotangent,
):
    hbm = pl.BlockSpec(memory_space=pltpu.HBM)
    vmem = pl.BlockSpec(memory_space=pltpu.VMEM)
    dma = pltpu.SemaphoreType.DMA
    out, gw, gb = pl.pallas_call(
        kernel,
        out_shape=(
            jax.ShapeDtypeStruct((ROWS, FEATS), BF16),
            jax.ShapeDtypeStruct((8, 16), F32),
            jax.ShapeDtypeStruct((1, FEATS), F32),
        ),
        in_specs=[hbm] * 13,
        out_specs=(vmem, vmem, vmem),
        scratch_shapes=[
            pltpu.VMEM((FEATS, FEATS), BF16),
            pltpu.VMEM((FEATS, FEATS), BF16),
            pltpu.VMEM((1, FEATS), F32),
            pltpu.VMEM((SLOTS, 16), jnp.int32),
            pltpu.VMEM((SLOTS, 16), jnp.int32),
            pltpu.VMEM((1, 16), jnp.int32),
            pltpu.VMEM((16, HALO), jnp.int32),
            pltpu.SMEM((1, 16), jnp.int32),
            pltpu.VMEM((16, HALO), F32),
            pltpu.VMEM((16, HALO), jnp.int32),
            pltpu.VMEM((16, ROWS, FEATS), BF16),
            pltpu.VMEM((16, SLOTS, TILE, TILE), BF16),
            pltpu.VMEM((ROWS, FEATS), BF16),
            pltpu.VMEM((4, TILE, FEATS), BF16),
            pltpu.VMEM((ROWS, 2 * FEATS), F32),
            pltpu.VMEM((FEATS, ROWS), BF16),
            pltpu.VMEM((16, PAY, HALO), BF16),
            pltpu.VMEM((16, PAY, HALO), BF16),
            pltpu.VMEM((16, 24, FEATS), F32),
            pltpu.VMEM((16, 24, FEATS), F32),
            pltpu.VMEM((16, 8, FEATS), F32),
            pltpu.VMEM((16, 8, FEATS), F32),
            pltpu.VMEM((16, HALO), F32),
            pltpu.VMEM((ROWS, FEATS), BF16),
            pltpu.VMEM((FEATS, ROWS), BF16),
            pltpu.VMEM((16, HALO), jnp.int32),
            pltpu.VMEM((16, HALO), F32),
            pltpu.VMEM((32, 16), jnp.int32),
            pltpu.SMEM((32, 16), jnp.int32),
            pltpu.VMEM((9, TILE, FEATS), F32),
            pltpu.VMEM((TILE, FEATS), F32),
            dma((16,)), dma((40,)), dma((64,)), dma((16,)), dma((16,)), dma((16,)), dma((16,)), dma((16,)), dma((16,)),
            dma((3,)), dma((3,)),
        ],
        compiler_params=pltpu.CompilerParams(
            collective_id=0, has_side_effects=True, vmem_limit_bytes=40 * 1024 * 1024
        ),
    )(*(pltpu.with_memory_space_constraint(value, pltpu.HBM) for value in (
        features.reshape(ROWS, FEATS),
        adj_tiles.reshape(16, SLOTS, TILE, TILE),
        cotangent.reshape(ROWS, FEATS),
        w_self,
        w_neigh,
        out_bias.reshape(1, FEATS),
        tile_rows.reshape(16, SLOTS).T,
        tile_cols.reshape(16, SLOTS).T,
        tile_count.reshape(1, 16),
        send_rows.reshape(16, HALO),
        send_count.reshape(1, 16),
        halo_weight.reshape(16, HALO),
        recv_rows.reshape(16, HALO),
    )))
    return out.reshape(1, 1, ROWS, FEATS), gw.T, gb.reshape(FEATS)


def solution(mesh):
    placed = (
        P("grp", "dom", None, None),
        P(),
        P(),
        P(),
        P("grp", "dom", None, None, None, None),
        P("grp", "dom", None, None),
        P("grp", "dom", None, None),
        P("grp", "dom", None),
        P("grp", "dom", None, None),
        P("grp", "dom", None),
        P("grp", "dom", None, None),
        P("grp", "dom", None, None),
        P("grp", "dom", None, None),
    )
    return jax.shard_map(
        local,
        mesh=mesh,
        in_specs=placed,
        out_specs=(P("grp", "dom", None, None), P("grp", "dom"), P()),
        check_vma=False,
    )
```

```python
import math

import jax
import jax.numpy as jnp
from jax import lax
from jax.experimental import pallas as pl
from jax.experimental.pallas import tpu as pltpu
from jax.sharding import PartitionSpec as P

MESH = pl.DeviceIdType.MESH
ROWS, FEATS, TILE, SLOTS, HALO = 512, 128, 128, 8, 256
SPLIT = 320
NZ = 8
PAY = FEATS + 16
BF16, F32 = jnp.bfloat16, jnp.float32


def dom_hops(j):
    dy, dx = j // 4, (j // 2) % 2
    return min(dy, 4 - dy) + 2 * dx


def grp_hops(j):
    dx, dz = j // NZ, j % NZ
    return min(dz, NZ - dz) + dx


DOM_FAR = sorted(range(1, 16), key=lambda j: -dom_hops(j))
GRP_FAR = sorted(range(1, 16), key=lambda j: -grp_hops(j))
REST = ROWS - SPLIT
PIECES = ((0, SPLIT), (SPLIT, REST), (SPLIT, REST // 2), (SPLIT + REST // 2, REST // 2))


def kernel(
    feat, adj, cot_in, wself_in, wneigh_in, bias_in, trows_in, tcols_in, tcount_in, srows_in, scount_in, hweight_in,
    rrows_in,
    out, gw, gb,
    wself, wneigh, bias, trows, tcols, tcount, srows, scount, hweight, rrows,
    part, adjv, cot, stage, acc, xt, hsend, hrecv, tbuf, rec1, tb2, rec2, wmask, fx, fxt, prows, pweight, table, plan, segment, degree,
    lsem, asend, arecv, hss, hrs, p1s, p1r, p2s, p2r, xs, xr,
):
    g, d = lax.axis_index("grp"), lax.axis_index("dom")
    xl, z = g // NZ, lax.rem(g, NZ)
    y, xh, core = d // 4, lax.rem(d // 2, 2), lax.rem(d, 2)
    up = xl * NZ + lax.rem(z + 1, NZ)
    down = xl * NZ + lax.rem(z + NZ - 1, NZ)
    side = (1 - xl) * NZ + z
    across = y * 4 + (1 - xh) * 2 + core

    def dom_to(j):
        dy, dx, dc = j // 4, lax.rem(j // 2, 2), lax.rem(j, 2)
        return lax.rem(y + dy, 4) * 4 + lax.rem(xh + dx, 2) * 2 + lax.rem(core + dc, 2)

    def grp_to(j):
        dx, dz = j // NZ, lax.rem(j, NZ)
        return lax.rem(xl + dx, 2) * NZ + lax.rem(z + dz, NZ)

    def halo_to(q):
        return lax.rem(y + q // 2, 4) * 4 + xh * 2 + lax.rem(core + lax.rem(q, 2), 2)

    def halo_from(slot):
        q = lax.rem(slot, 8)
        return lax.rem(y + 4 - q // 2, 4) * 4 + lax.rem(xh + slot // 8, 2) * 2 + lax.rem(core + lax.rem(q, 2), 2)

    def load(n, source, target):
        copy = pltpu.make_async_copy(source, target, lsem.at[n])
        copy.start()
        return copy

    load_x = load(0, feat, part.at[0])
    load_h = [load(1, srows_in, srows), load(2, scount_in, scount), load(3, hweight_in, hweight)]
    load_t = [load(4, trows_in, trows), load(5, tcols_in, tcols), load(6, tcount_in, tcount)]
    load_a = load(7, adj, adjv)
    load_r = load(8, rrows_in, rrows)
    load_w = [load(9, wself_in, wself), load(10, wneigh_in, wneigh), load(11, bias_in, bias), load(12, cot_in, cot)]

    barrier = pltpu.get_barrier_semaphore()
    for q in (4, 5, 2, 3, 6, 7, 1):
        pl.semaphore_signal(barrier, inc=1, device_id=(g, halo_to(q)), device_id_type=MESH)
    pl.semaphore_signal(barrier, inc=1, device_id=(g, across), device_id_type=MESH)
    for to in (up, down, side):
        pl.semaphore_signal(barrier, inc=1, device_id=(to, d), device_id_type=MESH)

    for copy in load_h:
        copy.wait()
    lane = lax.broadcasted_iota(jnp.int32, (1, HALO), 1)
    for j in range(16):
        wmask[j:j + 1, :] = jnp.where(lane < scount[0, j], hweight[j:j + 1, :], 0.0)
    load_x.wait()
    xt[...] = part[0].T
    acc[...] = jnp.zeros_like(acc)
    segment[8] = jnp.zeros((TILE, FEATS), F32)
    degree[...] = jnp.zeros((TILE, FEATS), F32)
    node = lax.broadcasted_iota(jnp.int32, (ROWS, HALO), 0)

    def build_halo(block, table, weights, to, target):
        pick = jnp.where(node == table[pl.ds(to, 1), :], 1.0, 0.0).astype(BF16)
        weight = weights[pl.ds(to, 1), :]
        rows = jnp.dot(block[...], pick, preferred_element_type=F32)
        target[0:FEATS, :] = (rows * weight).astype(BF16)
        target[FEATS:PAY, :] = jnp.broadcast_to(weight, (PAY - FEATS, HALO)).astype(BF16)

    def halo_copy(slot):
        return pltpu.make_async_remote_copy(
            src_ref=hsend.at[slot], dst_ref=hrecv.at[slot], send_sem=hss.at[slot], recv_sem=hrs.at[slot],
            device_id=(g, halo_to(lax.rem(slot, 8))), device_id_type=MESH,
        )

    def across_copy(n, source, target):
        return pltpu.make_async_remote_copy(
            src_ref=source, dst_ref=target, send_sem=xs.at[n], recv_sem=xr.at[n],
            device_id=(g, across), device_id_type=MESH,
        )

    sent = []

    def send(slot_from, slot_to, piece, to):
        n = len(sent)
        rows = pl.ds(*PIECES[piece])
        copy = pltpu.make_async_remote_copy(
            src_ref=part.at[slot_from, rows, :], dst_ref=part.at[slot_to, rows, :],
            send_sem=asend.at[n], recv_sem=arecv.at[4 * slot_to + piece],
            device_id=(to, d), device_id_type=MESH,
        )
        copy.start()
        sent.append(copy)

    def landed(slot, piece):
        rows = pl.ds(*PIECES[piece])
        pltpu.make_async_remote_copy(
            src_ref=part.at[slot, rows, :], dst_ref=part.at[slot, rows, :],
            send_sem=asend.at[0], recv_sem=arecv.at[4 * slot + piece],
            device_id=(up, d), device_id_type=MESH,
        ).wait_recv()

    def sort_slots():
        count = tcount[...]
        keys = [jnp.where(count > s, trows[s:s + 1, :], 4) for s in range(SLOTS)]
        one = jnp.ones((1, 16), jnp.int32)
        none = jnp.zeros((1, 16), jnp.int32)
        rank = []
        for s in range(SLOTS):
            total = none
            for t in range(SLOTS):
                if t != s:
                    ahead = keys[t] <= keys[s] if t < s else keys[t] < keys[s]
                    total += jnp.where(ahead, one, none)
            rank.append(total)
        for i in range(SLOTS):
            at, column, key = none, none, none
            for s in range(SLOTS):
                here = rank[s] == i
                at += jnp.where(here, s * one, none)
                column += jnp.where(here, tcols[s:s + 1, :], none)
                key += jnp.where(here, keys[s], none)
            table[i:i + 1, :] = at
            table[8 + i:9 + i, :] = column
            table[16 + i:17 + i, :] = key
        for r in range(4):
            upto, equal = none, none
            for s in range(SLOTS):
                upto += jnp.where(keys[s] <= r, one, none)
                equal += jnp.where(keys[s] == r, one, none)
            table[24 + r:25 + r, :] = jnp.where(equal > 0, upto - 1, 8)
        copy = pltpu.make_async_copy(table, plan, lsem.at[13])
        copy.start()
        return copy

    lane16 = lax.broadcasted_iota(jnp.int32, (16, FEATS), 1)

    def absorb(slot, source):
        stage[...] = part[slot].reshape(4, TILE, FEATS)
        running, before, tiles, marks = None, None, [], []
        for i in range(SLOTS):
            tile = adjv[source, plan[i, source]]
            product = jnp.dot(tile, stage[plan[8 + i, source]], preferred_element_type=F32)
            key = jnp.full((16, FEATS), plan[16 + i, source], jnp.int32)
            tiles.append(tile)
            marks += [jnp.where(lane16 == key, 1.0, 0.0).astype(BF16)] * (TILE // 16)
            if i:
                same = jnp.concatenate([jnp.where(key == before, 1, 0)] * (TILE // 16), axis=0) > 0
                product += jnp.where(same, running, 0.0)
            running, before = product, key
            segment[i] = running
        degree[...] += jnp.dot(
            jnp.concatenate(tiles, axis=1), jnp.concatenate(marks, axis=0), preferred_element_type=F32
        )
        for r in range(4):
            acc[r * TILE:(r + 1) * TILE, 0:FEATS] += segment[plan[24 + r, source]]

    def absorb_pair(first, dist, column):
        def body(k, _):
            absorb(first + k, column * NZ + lax.rem(z + NZ + dist * (2 * k - 1), NZ))
            return 0
        lax.fori_loop(0, 2, body, 0)

    def take_halo(*slots):
        for slot in slots:
            if slot != 8:
                halo_copy(slot).wait_recv()
        hits = jnp.concatenate(
            [jnp.where(node == rrows[pl.ds(halo_from(slot), 1), :], 1.0, 0.0).astype(BF16) for slot in slots], axis=1
        )
        rows = jnp.concatenate([hrecv[slot] for slot in slots], axis=1)
        acc[:, 0:PAY] += lax.dot_general(hits, rows, (((1,), (1,)), ((), ())), preferred_element_type=F32)

    pl.semaphore_wait(barrier, 11)

    send(0, 1, 1, side)
    send(0, 2, 0, up)
    send(0, 3, 0, down)
    crossing = [
        across_copy(0, srows, prows), across_copy(1, wmask, pweight), across_copy(2, part.at[0], fx),
    ]
    for copy in crossing:
        copy.start()
    send(0, 2, 1, up)
    send(0, 3, 1, down)
    send(0, 1, 0, side)

    @pl.loop(1, 8)
    def _(q):
        build_halo(xt, srows, wmask, halo_to(q), hsend.at[q])
        halo_copy(q).start()

    for copy in load_t:
        copy.wait()
    planned = sort_slots()
    other = 1 - xl
    landed(2, 0)
    send(2, 6, 0, up)
    landed(3, 0)
    send(3, 7, 0, down)
    send(2, 4, 0, side)
    send(3, 5, 0, side)
    landed(1, 1)
    send(1, 4, 1, up)
    send(1, 5, 1, down)
    load_a.wait()
    load_r.wait()
    planned.wait()
    absorb(0, g)
    landed(2, 1)
    send(2, 6, 1, up)
    landed(3, 1)
    send(3, 7, 1, down)
    for copy in crossing:
        copy.wait_recv()
    fxt[...] = fx[...].T

    @pl.loop(1, 8)
    def _(q):
        build_halo(fxt, prows, pweight, halo_to(q), hsend.at[8 + q])
        halo_copy(8 + q).start()

    landed(6, 0)
    send(6, 10, 0, up)
    landed(7, 0)
    send(7, 11, 0, down)
    send(6, 8, 0, side)
    send(7, 9, 0, side)
    absorb_pair(2, 1, xl)
    landed(4, 1)
    send(4, 8, 1, up)
    landed(5, 1)
    send(5, 9, 1, down)
    landed(1, 0)
    absorb(1, side)
    build_halo(fxt, prows, pweight, halo_to(0), hrecv.at[8])
    landed(6, 1)
    send(6, 10, 1, up)
    landed(7, 1)
    send(7, 11, 1, down)
    absorb_pair(6, 2, xl)
    take_halo(1, 2)
    landed(10, 0)
    send(10, 14, 0, up)
    send(10, 12, 0, side)
    landed(11, 0)
    send(11, 13, 0, side)
    landed(4, 0)
    landed(5, 0)
    absorb_pair(4, 1, other)
    take_halo(3, 4)
    landed(8, 1)
    send(8, 12, 1, up)
    landed(9, 1)
    send(9, 13, 1, down)
    take_halo(5, 6)
    take_halo(7, 8)
    landed(10, 1)
    landed(11, 1)
    send(11, 14, 1, down)
    absorb_pair(10, 3, xl)
    take_halo(9, 10)
    landed(14, 0)
    send(14, 15, 0, side)
    landed(8, 0)
    landed(9, 0)
    absorb_pair(8, 2, other)
    take_halo(11, 12)
    landed(12, 1)
    send(12, 15, 2, up)
    landed(13, 1)
    send(13, 15, 3, down)
    landed(14, 1)
    absorb(14, xl * NZ + lax.rem(z + 4, NZ))
    take_halo(13, 14)
    landed(12, 0)
    landed(13, 0)
    absorb_pair(12, 3, other)
    take_halo(15)
    landed(15, 2)
    landed(15, 3)
    landed(15, 0)
    absorb(15, other * NZ + lax.rem(z + 4, NZ))

    for copy in load_w:
        copy.wait()
    wcat = jnp.concatenate([wself[...], wneigh[...]], axis=0)
    bias_row = bias[...]
    total_b = jnp.zeros((1, FEATS), F32)
    total_w = jnp.zeros((FEATS, 2 * FEATS), F32)
    for r in range(4):
        rs = pl.ds(r * TILE, TILE)
        total = jnp.broadcast_to(1.0 + acc[rs, FEATS:FEATS + 1] + degree[:, r:r + 1], (TILE, FEATS))
        agg = (acc[rs, 0:FEATS] * lax.rsqrt(total)).astype(BF16)
        cat = jnp.concatenate([part[0, rs, :], agg], axis=1)
        pre = jnp.dot(cat, wcat, preferred_element_type=F32) + bias_row
        sig = jax.nn.sigmoid(pre)
        out[rs, :] = (pre * sig).astype(BF16)
        slope = (cot[rs, :].astype(F32) * sig * (1.0 + pre * (1.0 - sig))).astype(BF16)
        total_b += jnp.sum(slope.astype(F32), axis=0, keepdims=True)
        total_w += lax.dot_general(slope, cat, (((0,), (0,)), ((), ())), preferred_element_type=F32)
    tbuf[:, 0:8, :] = total_w[:, 0:FEATS].reshape(16, 8, FEATS)
    tbuf[:, 8:16, :] = total_w[:, FEATS:].reshape(16, 8, FEATS)
    tbuf[:, 16:24, :] = jnp.broadcast_to(total_b[None], (16, 8, FEATS))

    def first_copy(j):
        return pltpu.make_async_remote_copy(
            src_ref=tbuf.at[dom_to(j), pl.ds(0, 17), :], dst_ref=rec1.at[j, pl.ds(0, 17), :],
            send_sem=p1s.at[j], recv_sem=p1r.at[j],
            device_id=(g, dom_to(j)), device_id_type=MESH,
        )

    def second_copy(j):
        return pltpu.make_async_remote_copy(
            src_ref=tb2.at[grp_to(j), pl.ds(0, 2), :], dst_ref=rec2.at[j, pl.ds(0, 2), :],
            send_sem=p2s.at[j], recv_sem=p2r.at[j],
            device_id=(grp_to(j), d), device_id_type=MESH,
        )

    for j in DOM_FAR:
        first_copy(j).start()

    for copy in sent + crossing:
        copy.wait_send()

    @pl.loop(1, 8)
    def _(q):
        halo_copy(q).wait_send()
        halo_copy(8 + q).wait_send()

    red_w, red_b = tbuf[d, 0:16, :], tbuf[d, 16:17, :]
    for j in DOM_FAR[::-1]:
        first_copy(j).wait_recv()
        red_w += rec1[j, 0:16, :]
        red_b += rec1[j, 16:17, :]

    row8 = lax.broadcasted_iota(jnp.int32, (8, FEATS), 0)
    block16 = lax.broadcasted_iota(jnp.int32, (8, FEATS), 1) // 16
    for half in range(2):
        tile = red_w[8 * half:8 * half + 8]
        turned = jnp.zeros((8, FEATS), F32)
        for k in range(8):
            moved = tile if k == 0 else pltpu.roll(tile, 16 * k, 1)
            moved = jnp.where(row8 == block16, moved, 0.0)
            turned += moved if k == 0 else pltpu.roll(moved, 8 - k, 0)
        for p in range(8):
            tb2[8 * half + p, 0:1, :] = turned[p:p + 1]
            tb2[8 * half + p, 1:2, :] = red_b
    for j in GRP_FAR:
        second_copy(j).start()
    fin = tb2[g, 0:2, :]
    for j in GRP_FAR[::-1]:
        second_copy(j).wait_recv()
        fin += rec2[j, 0:2, :]
    fin *= 1.0 / math.sqrt(ROWS * 256)
    for c in range(8):
        gw[c:c + 1, :] = fin[0:1, 16 * c:16 * c + 16]
    gb[...] = fin[1:2]

    @pl.loop(1, 16)
    def _(j):
        first_copy(j).wait_send()
        second_copy(j).wait_send()


def local(
    features, w_self, w_neigh, out_bias, adj_tiles, tile_rows, tile_cols, tile_count, send_rows,
    send_count, halo_weight, recv_rows, cotangent,
):
    hbm = pl.BlockSpec(memory_space=pltpu.HBM)
    vmem = pl.BlockSpec(memory_space=pltpu.VMEM)
    dma = pltpu.SemaphoreType.DMA
    out, gw, gb = pl.pallas_call(
        kernel,
        out_shape=(
            jax.ShapeDtypeStruct((ROWS, FEATS), BF16),
            jax.ShapeDtypeStruct((8, 16), F32),
            jax.ShapeDtypeStruct((1, FEATS), F32),
        ),
        in_specs=[hbm] * 13,
        out_specs=(vmem, vmem, vmem),
        scratch_shapes=[
            pltpu.VMEM((FEATS, FEATS), BF16),
            pltpu.VMEM((FEATS, FEATS), BF16),
            pltpu.VMEM((1, FEATS), F32),
            pltpu.VMEM((SLOTS, 16), jnp.int32),
            pltpu.VMEM((SLOTS, 16), jnp.int32),
            pltpu.VMEM((1, 16), jnp.int32),
            pltpu.VMEM((16, HALO), jnp.int32),
            pltpu.SMEM((1, 16), jnp.int32),
            pltpu.VMEM((16, HALO), F32),
            pltpu.VMEM((16, HALO), jnp.int32),
            pltpu.VMEM((16, ROWS, FEATS), BF16),
            pltpu.VMEM((16, SLOTS, TILE, TILE), BF16),
            pltpu.VMEM((ROWS, FEATS), BF16),
            pltpu.VMEM((4, TILE, FEATS), BF16),
            pltpu.VMEM((ROWS, 2 * FEATS), F32),
            pltpu.VMEM((FEATS, ROWS), BF16),
            pltpu.VMEM((16, PAY, HALO), BF16),
            pltpu.VMEM((16, PAY, HALO), BF16),
            pltpu.VMEM((16, 24, FEATS), F32),
            pltpu.VMEM((16, 24, FEATS), F32),
            pltpu.VMEM((16, 8, FEATS), F32),
            pltpu.VMEM((16, 8, FEATS), F32),
            pltpu.VMEM((16, HALO), F32),
            pltpu.VMEM((ROWS, FEATS), BF16),
            pltpu.VMEM((FEATS, ROWS), BF16),
            pltpu.VMEM((16, HALO), jnp.int32),
            pltpu.VMEM((16, HALO), F32),
            pltpu.VMEM((32, 16), jnp.int32),
            pltpu.SMEM((32, 16), jnp.int32),
            pltpu.VMEM((9, TILE, FEATS), F32),
            pltpu.VMEM((TILE, FEATS), F32),
            dma((16,)), dma((40,)), dma((64,)), dma((16,)), dma((16,)), dma((16,)), dma((16,)), dma((16,)), dma((16,)),
            dma((3,)), dma((3,)),
        ],
        compiler_params=pltpu.CompilerParams(
            collective_id=0, has_side_effects=True, vmem_limit_bytes=40 * 1024 * 1024
        ),
    )(*(pltpu.with_memory_space_constraint(value, pltpu.HBM) for value in (
        features.reshape(ROWS, FEATS),
        adj_tiles.reshape(16, SLOTS, TILE, TILE),
        cotangent.reshape(ROWS, FEATS),
        w_self,
        w_neigh,
        out_bias.reshape(1, FEATS),
        tile_rows.reshape(16, SLOTS).T,
        tile_cols.reshape(16, SLOTS).T,
        tile_count.reshape(1, 16),
        send_rows.reshape(16, HALO),
        send_count.reshape(1, 16),
        halo_weight.reshape(16, HALO),
        recv_rows.reshape(16, HALO),
    )))
    return out.reshape(1, 1, ROWS, FEATS), gw.T, gb.reshape(FEATS)


def solution(mesh):
    placed = (
        P("grp", "dom", None, None),
        P(),
        P(),
        P(),
        P("grp", "dom", None, None, None, None),
        P("grp", "dom", None, None),
        P("grp", "dom", None, None),
        P("grp", "dom", None),
        P("grp", "dom", None, None),
        P("grp", "dom", None),
        P("grp", "dom", None, None),
        P("grp", "dom", None, None),
        P("grp", "dom", None, None),
    )
    return jax.shard_map(
        local,
        mesh=mesh,
        in_specs=placed,
        out_specs=(P("grp", "dom", None, None), P("grp", "dom"), P()),
        check_vma=False,
    )
```
